32 devices in a mesh: oct: 2 (over core), sub: 16 (over z, y, x).
Axes of the slice: x: 2, y: 2, z: 4, core: 2. Of those that a mesh axis runs over, the one named last changes fastest.
Arguments:
- coefficients: float32 [512, 4096], P(('oct', 'sub')), may hold values from -6 to 6
- potential: float32 [512, 4096], P(('oct', 'sub')), may hold values from 0.2 to 2
- to_values: float32 [16, 16], replicated, may hold values from -1.5 to 1.5
- x_kernels: bfloat16 [20, 48, 16], replicated, may hold values from -0.5 to 0.5
- yz_kernels: bfloat16 [256, 46080], replicated, may hold values from -0.046875 to 0.046875
- two_scale: float32 [2, 16, 16], replicated, may hold values from -1 to 1
- disp_ids: int32 [512, 16], P(('oct', 'sub')), may hold values from -1 to 26, as said below
- dest_box: int32 [512, 16], P(('oct', 'sub')), may hold values from -1 to 511, as said below
- parent_of: int32 [512], P(('oct', 'sub')), may hold values from 0 to 63, as said below
- child_octant: int32 [512], P(('oct', 'sub')), may hold values from 0 to 7
Outputs:
- next_field: float32 [512, 4096], P(('oct', 'sub'))
- parents: float32 [64, 4096], P(('oct', 'sub'))
The draws below stay inside these ranges and needn't reach their ends.
Inputs may be any that keep to these rules, and one draw needn't show every extreme that they name: `disp_ids`: -1 marks an empty slot, exactly where dest_box is -1; in every row the live slots come first, 4 or more of them. `dest_box`: among the live slots of one aligned block of 16 rows, at most 8 name boxes of any one aligned block of 16 boxes; some box block receives exactly 8 from every row block. Every parent is named by exactly 8 boxes, whose child_octant values are 0 to 7; parent_of[b] // 32 == b // 256. Within one aligned block of 16 boxes, at most 1 box has its parent in any one aligned block of 2 parents, and some parent block is named by exactly 1 of them.
All inputs are finite; a program needn't handle non-finite values.
Results may differ from the reference program's by a relative error of at most 0.018.
Values may be sent and summed in bfloat16 or wider, within the bound.
No kernel may reach another device: no remote copies, remote signals or barrier semaphores. Data moves between devices by JAX's collectives and lax.ppermute only.
A program may use at most 192 MiB of HBM per device.

```python
import math
import jax
import jax.numpy as jnp
from jax import lax

K = 16
TERMS = 20
LIST = 16
ITERS = 2
BOX_DEV = 16
BOXES = 512
GROUP_BOXES = 256
PARENTS = 64
CAP = 8
N_OCT = 2
N_SUB = 16


def route_tables(key):
    base = jax.random.fold_in(key, 7)
    key_len, key_perm, key_pick, key_disp, key_local = jax.random.split(base, 5)
    devices_all = N_OCT * N_SUB
    lengths = jax.random.randint(key_len, (devices_all, BOX_DEV, 1), LIST // 4, LIST + 1)
    slot_ids = jnp.arange(LIST, dtype=jnp.int32)
    is_live = slot_ids[None, None, :] < lengths
    position = slot_ids[None, :] * BOX_DEV + jnp.arange(BOX_DEV, dtype=jnp.int32)[:, None]
    group_ids = position // CAP
    target = jax.random.randint(key_pick, (), 0, devices_all)
    orderings = jax.vmap(lambda single: jax.random.permutation(single, devices_all))(jax.random.split(key_perm, devices_all))
    leading = orderings[:, :1]
    orderings = jnp.where(orderings == target, leading, orderings)
    orderings = orderings.at[:, 0].set(target)
    owners = orderings[:, group_ids]
    local_ids = jax.random.randint(key_local, (devices_all, BOX_DEV, LIST), 0, BOX_DEV)
    dest_ids = jnp.where(is_live, owners * BOX_DEV + local_ids, -1)
    disp_vals = jnp.where(is_live, jax.random.randint(key_disp, (devices_all, BOX_DEV, LIST), 0, 27), -1)
    return (disp_vals.reshape(BOXES, LIST).astype(jnp.int32), dest_ids.reshape(BOXES, LIST).astype(jnp.int32))


def group_tree(key_shift, key_rank, key_place):
    parent_local = BOX_DEV // 8
    slots = jnp.arange(BOX_DEV, dtype=jnp.int32)
    shift_ids = jnp.arange(N_SUB, dtype=jnp.int32)
    scores = jax.random.permutation(key_shift, N_SUB).astype(jnp.int32)
    forced = (shift_ids == 1) | (shift_ids == N_SUB - 1) | (shift_ids == N_SUB // 2)
    scores = jnp.where(forced, scores - N_SUB, scores)
    shift_order = jnp.argsort(scores, stable=True).astype(jnp.int32)
    shifts = shift_order[slots % N_SUB]
    senders = jnp.arange(N_SUB, dtype=jnp.int32)[:, None]
    owners = (senders + shifts[None, :]) % N_SUB
    ranks = jax.vmap(lambda single: jax.random.permutation(single, BOX_DEV))(jax.random.split(key_rank, N_SUB)).astype(jnp.int32)
    rank_at = ranks[owners, slots[None, :]]
    parent_vals = owners * parent_local + rank_at // 8
    octant_vals = rank_at % 8
    places = jax.vmap(lambda single: jax.random.permutation(single, BOX_DEV))(jax.random.split(key_place, N_SUB)).astype(jnp.int32)
    blank = jnp.zeros((N_SUB, BOX_DEV), jnp.int32)
    parent_rows = blank.at[senders, places].set(parent_vals)
    octant_rows = blank.at[senders, places].set(octant_vals)
    return (parent_rows.reshape(GROUP_BOXES), octant_rows.reshape(GROUP_BOXES))


def tree_tables(key):
    base = jax.random.fold_in(key, 11)
    key_shift, key_rank, key_place = jax.random.split(base, 3)
    parent_rows, octant_rows = jax.vmap(group_tree)(jax.random.split(key_shift, N_OCT), jax.random.split(key_rank, N_OCT), jax.random.split(key_place, N_OCT))
    offsets = jnp.arange(N_OCT, dtype=jnp.int32)[:, None] * (GROUP_BOXES // 8)
    parent_rows = parent_rows + offsets
    return (parent_rows.reshape(BOXES).astype(jnp.int32), octant_rows.reshape(BOXES).astype(jnp.int32))


def draw_disp_ids(key, part):
    return route_tables(key)[0]


def draw_dest_box(key, part):
    return route_tables(key)[1]


def draw_parent_of(key, part):
    return tree_tables(key)[0]


def draw_child_octant(key, part):
    return tree_tables(key)[1]


def levels(stream_key, extent, cuts, least, top_value):
    gain = 1.0
    for dim, parts in cuts:
        heights = jax.random.uniform(jax.random.fold_in(jax.random.fold_in(stream_key, 6), dim), (parts,), jnp.float32, least / len(cuts), top_value / len(cuts))
        gain = gain * jnp.repeat(jnp.exp(heights), extent[dim] // parts).reshape((-1,) + (1,) * (len(extent) - 1 - dim))
    return gain


def bell_draw(stream_key, extent, deviation, reach, cuts=(), kind=jnp.bfloat16):
    values = deviation * jax.random.normal(stream_key, extent, jnp.float32)
    if cuts:
        values = values * levels(stream_key, extent, cuts, -0.22, 0.18)
    return jnp.clip(values, -reach, reach).astype(kind)


def setup_inputs(seed: int = 0) -> dict:
    seeds = jax.random.split(jax.random.key(seed), 11)
    return {
        "coefficients": bell_draw(seeds[0], (BOXES, K**3), 1.0, 6.0, ((0, 32),), jnp.float32),
        "potential": jnp.clip(jnp.exp(math.log(2.0) - 2.3025851 * jax.random.uniform(seeds[1], (BOXES, K**3), jnp.float32) ** levels(seeds[1], (BOXES, K**3), ((0, 32),), -0.2, 0.2)), 0.2, 2.0),
        "to_values": bell_draw(seeds[2], (K, K), K ** -0.5, 1.5, (), jnp.float32),
        "x_kernels": bell_draw(seeds[3], (TERMS, 3 * K, K), (8 * K) ** -0.5, 0.5),
        "yz_kernels": bell_draw(seeds[4], (K * K, TERMS * 9 * K * K), (64 * K * K) ** -0.5, 0.046875),
        "two_scale": bell_draw(seeds[5], (2, K, K), (2 * K) ** -0.5, 1.0, (), jnp.float32),
        "disp_ids": draw_disp_ids(jax.random.fold_in(seeds[10], 71), 0),
        "dest_box": draw_dest_box(jax.random.fold_in(seeds[10], 71), 0),
        "parent_of": draw_parent_of(jax.random.fold_in(seeds[10], 71), 0),
        "child_octant": draw_child_octant(jax.random.fold_in(seeds[10], 71), 0),
    }


def transform_three(blocks, along_x, along_y, along_z):
    highest = lax.Precision.HIGHEST
    cube_view = blocks.reshape(blocks.shape[0], K, K, K)
    cube_view = jnp.einsum("ix,bxyz->biyz", along_x, cube_view, precision=highest)
    cube_view = jnp.einsum("jy,biyz->bijz", along_y, cube_view, precision=highest)
    cube_view = jnp.einsum("kz,bijz->bijk", along_z, cube_view, precision=highest)
    return cube_view.reshape(blocks.shape[0], K ** 3)


def lift_each(blocks, filters, octant):
    highest = lax.Precision.HIGHEST
    along_x = filters[octant // 4]
    along_y = filters[(octant // 2) % 2]
    along_z = filters[octant % 2]
    cube_view = blocks.reshape(blocks.shape[0], K, K, K)
    cube_view = jnp.einsum("bix,bxyz->biyz", along_x, cube_view, precision=highest)
    cube_view = jnp.einsum("bjy,biyz->bijz", along_y, cube_view, precision=highest)
    cube_view = jnp.einsum("bkz,bijz->bijk", along_z, cube_view, precision=highest)
    return cube_view.reshape(blocks.shape[0], K ** 3)


def reference(coefficients, potential, to_values, x_kernels, yz_kernels, two_scale, disp_ids, dest_box, parent_of, child_octant):
    highest = lax.Precision.HIGHEST
    plane_size = K * K
    cube_size = K ** 3
    block_boxes = 16
    count_blocks = BOXES // block_boxes
    x_wide = x_kernels.astype(jnp.float32)
    flipped = jnp.swapaxes(two_scale, 1, 2)
    current = coefficients
    parents = jnp.zeros((PARENTS, cube_size), jnp.float32)
    for iteration in range(ITERS):
        values = transform_three(current, to_values, to_values, to_values)
        product = values * (potential + 0.25 * values * values)
        source = transform_three(product, to_values.T, to_values.T, to_values.T).astype(jnp.bfloat16)

        def convolve(running, block_items):
            source_blk, disp_blk, dest_blk = block_items
            partial_value = jnp.dot(source_blk.reshape(block_boxes * K, plane_size), yz_kernels, preferred_element_type=jnp.float32).astype(jnp.bfloat16)
            partial_value = lax.optimization_barrier(partial_value).astype(jnp.float32).reshape(block_boxes, K, TERMS, 9 * plane_size)
            convolved = jnp.einsum("bxmr,max->bar", partial_value, x_wide, precision=highest)
            convolved = convolved.reshape(block_boxes, 3, K, 9, plane_size).transpose(0, 1, 3, 2, 4).reshape(block_boxes, 27, cube_size)
            picked = jnp.take_along_axis(convolved, jnp.maximum(disp_blk, 0)[:, :, None], axis=1).astype(jnp.bfloat16)
            picked = lax.optimization_barrier(picked).astype(jnp.float32)
            target = jnp.where(dest_blk < 0, BOXES, dest_blk).reshape(-1)
            running = running.at[target].add(picked.reshape(-1, cube_size), mode="drop")
            return running, None

        gathered, unused = lax.scan(
            convolve,
            jnp.zeros((BOXES, cube_size), jnp.float32),
            (source.reshape(count_blocks, block_boxes, cube_size),
             disp_ids.reshape(count_blocks, block_boxes, LIST),
             dest_box.reshape(count_blocks, block_boxes, LIST)))
        lifted = lift_each(gathered, two_scale, child_octant)
        parents = jnp.zeros((PARENTS, cube_size), jnp.float32).at[parent_of].add(lifted)
        current = gathered - lift_each(parents[parent_of], flipped, child_octant)
    return current, parents
```

```python
import functools

import jax
import jax.numpy as jnp
from jax import lax
from jax.experimental import pallas as pl
from jax.experimental.pallas import tpu as pltpu
from jax.sharding import Mesh
from jax.sharding import PartitionSpec as P

ITERS = 2
BLOCK = 32
GROUP = 4
MIB = 1024 * 1024


def mm(left, right):
    return jnp.dot(left, right, precision=lax.Precision.HIGHEST, preferred_element_type=jnp.float32)


def rows_high(matrix):
    order_k, width = matrix.shape
    return jnp.broadcast_to(matrix[:, None, :], (order_k, order_k, width)).reshape(order_k * order_k, width)


def rows_low(matrix):
    order_k, width = matrix.shape
    return jnp.broadcast_to(matrix[None, :, :], (order_k, order_k, width)).reshape(order_k * order_k, width)


def spread_columns(matrix):
    order_k = matrix.shape[0]
    shape = (order_k, order_k * order_k)
    slot = lax.broadcasted_iota(jnp.int32, shape, 0)
    lane = lax.broadcasted_iota(jnp.int32, shape, 1)
    high = (lane // order_k == slot).astype(jnp.float32)
    low = (lane % order_k == slot).astype(jnp.float32)
    return mm(matrix, high), mm(matrix, low)


def masks(order_k):
    shape = (order_k * order_k, order_k * order_k)
    row = lax.broadcasted_iota(jnp.int32, shape, 0)
    lane = lax.broadcasted_iota(jnp.int32, shape, 1)
    return row // order_k, row % order_k, lane // order_k, lane % order_k


def first_kernel(coef_ref, pot_ref, to_ref, back_ref, out_ref):
    order_k = to_ref.shape[0]
    plane = order_k * order_k
    to_high, to_low = spread_columns(to_ref[...])
    back_high, back_low = spread_columns(back_ref[...])
    row_high, row_low, lane_high, lane_low = masks(order_k)
    value_pair = rows_high(back_high) * rows_low(back_low)
    back_pair = rows_high(to_high) * rows_low(to_low)
    value_x = jnp.where(row_low == lane_low, rows_high(to_high), 0.0)
    source_x = jnp.where(row_high == lane_low, rows_low(back_high), 0.0)

    def by_x(ref):
        return jnp.concatenate([ref[:, x * plane : (x + 1) * plane] for x in range(order_k)], axis=0)

    values = mm(value_x, mm(by_x(coef_ref), value_pair))
    product = values * (by_x(pot_ref) + 0.25 * values * values)
    source = mm(source_x, mm(product, back_pair))
    out_ref[...] = source.astype(jnp.bfloat16).reshape(out_ref.shape)


def tree_kernel(last, part_count, *refs):
    parts = refs[:part_count]
    two_ref, flip_ref = refs[part_count : part_count + 2]
    rest = refs[part_count + 2 :]
    order_k = two_ref.shape[1]
    plane = order_k * order_k
    gathered = parts[0][...].astype(jnp.float32)
    for part in parts[1:]:
        gathered = gathered + part[...].astype(jnp.float32)
    boxes = gathered.shape[0]
    parent_count = boxes // 8

    def stacked(quad):
        return jnp.concatenate(
            [gathered[8 * p + 4 * c + quad] for p in range(parent_count) for c in range(2)], axis=0
        )

    two = [spread_columns(two_ref[c]) for c in range(2)]
    flip = [spread_columns(flip_ref[c]) for c in range(2)]
    summed = None
    for quad in range(4):
        lift = rows_high(flip[quad // 2][0]) * rows_low(flip[quad % 2][1])
        inner = mm(stacked(quad), lift)
        summed = inner if summed is None else summed + inner
    own = []
    dropped_x = []
    for p in range(parent_count):
        total = None
        for c in range(2):
            start = (2 * p + c) * order_k
            part = mm(two_ref[c], summed[start : start + order_k])
            total = part if total is None else total + part
        own.append(total)
        dropped_x += [mm(flip_ref[c], total) for c in range(2)]
    dropped_x = jnp.concatenate(dropped_x, axis=0)
    dropped = []
    for quad in range(4):
        drop = rows_high(two[quad // 2][0]) * rows_low(two[quad % 2][1])
        dropped.append(mm(dropped_x, drop))
    fields = []
    for b in range(boxes):
        p, c, quad = b // 8, (b // 4) % 2, b % 4
        start = (2 * p + c) * order_k
        fields.append(gathered[b] - dropped[quad][start : start + order_k])
    if last:
        pick_ref, field_ref, parent_ref, held = rest
        for b in range(boxes):
            held[b] = fields[b]
        for s in range(field_ref.shape[0]):
            field_ref[s] = held[pick_ref[s]]
        for p in range(parent_count):
            for i in range(order_k):
                parent_ref[p : p + 1, i * plane : (i + 1) * plane] = own[p][i : i + 1]
    else:
        pot_ref, to_ref, back_ref, out_ref = rest
        to_high, to_low = spread_columns(to_ref[...])
        back_high, back_low = spread_columns(back_ref[...])
        row_high, row_low, lane_high, lane_low = masks(order_k)
        value_pair = rows_high(back_high) * rows_low(back_low)
        back_pair = rows_high(to_high) * rows_low(to_low)
        value_x = jnp.where(row_high == lane_high, rows_low(to_low), 0.0)
        source_x = jnp.where(row_high == lane_high, rows_low(back_low), 0.0)
        current = jnp.concatenate(fields, axis=0)
        values = mm(value_x, mm(current, value_pair))
        product = values * (pot_ref[...].reshape(values.shape) + 0.25 * values * values)
        source = mm(source_x, mm(product, back_pair))
        out_ref[...] = source.astype(jnp.bfloat16).reshape(out_ref.shape)


def conv_kernel(dims, packed, offs, *refs):
    term_count, order_k, disp_count, source_count, dest_count = dims
    source_refs = refs[:source_count]
    xl_ref, w_hbm = refs[source_count : source_count + 2]
    out_refs = refs[source_count + 2 : source_count + 2 + dest_count]
    wbuf, pbuf, total, held, sems, held_sems = refs[source_count + 2 + dest_count :]
    plane = order_k * order_k
    half = term_count // 2
    depth = term_count * order_k
    block_boxes = out_refs[0].shape[0]
    dest_rows = dest_count * block_boxes
    loads = [
        pltpu.make_async_copy(ref, held.at[pl.ds(n * block_boxes, block_boxes)], held_sems.at[n])
        for n, ref in enumerate(source_refs)
    ]
    for load in loads:
        load.start()
    for ll in range(disp_count):
        for m in range(term_count):
            pltpu.make_async_copy(
                w_hbm.at[:, pl.ds((m * disp_count + ll) * plane, plane)], wbuf.at[ll, m], sems.at[ll]
            ).start()
    total[...] = jnp.zeros_like(total)
    for load in loads:
        load.wait()

    def push_w(ll, j, reg):
        pltpu.matmul_push_rhs(wbuf[ll, j], reg, 0)
        pltpu.matmul_push_rhs(wbuf[ll, half + j], reg, 1)

    def block_body(ll, base, live, slots):
        pl.run_scoped(
            functools.partial(with_accs, ll, base, live, slots),
            *[
                [[pltpu.ACC(unit)((order_k, plane), jnp.float32) for _ in range(slots)] for _ in range(2)]
                for unit in range(2)
            ],
        )

    def with_accs(ll, base, live, slots, *accs):
        codes = [packed[base + t] for t in range(slots)]
        ids = [code // (4 * dest_rows) for code in codes]
        shifts = [(code // dest_rows) % 4 for code in codes]

        def acc(par):
            for t in range(slots):
                lhs = held[ids[t]]
                for unit in range(2):
                    pltpu.matmul_acc_lhs(accs[unit][par][t], lhs, par if t == 0 else None)

        def pop(par, j):
            for t in range(slots):
                for unit in range(2):
                    row = pl.multiple_of((unit * half + j) * order_k + t * depth, order_k)
                    pbuf[pl.ds(row, order_k), :] = pltpu.matmul_pop(accs[unit][par][t]).astype(jnp.bfloat16)

        push_w(ll, 0, 0)
        acc(0)
        push_w(ll, 1, 1)

        def pair(g, carry):
            j = 2 * g
            acc(1)
            push_w(ll, j + 2, 0)
            pop(0, j)
            acc(0)
            push_w(ll, j + 3, 1)
            pop(1, j + 1)
            return carry

        lax.fori_loop(0, half // 2 - 1, pair, 0)
        acc(1)
        pop(0, half - 2)
        pop(1, half - 1)

        tiles = GROUP * depth // plane
        for g in range(slots // GROUP):
            unit = g % 2
            for q in range(tiles):
                reg = q % 2
                pltpu.matmul_push_rhs(pbuf[pl.ds(g * GROUP * depth + q * plane, plane), :], reg, unit)
                first = True
                for s in range(GROUP):
                    if s * depth < (q + 1) * plane and (s + 1) * depth > q * plane:
                        t = g * GROUP + s
                        pltpu.matmul_acc_lhs(
                            accs[unit][0][t], xl_ref[shifts[t], q + s], reg if first else None
                        )
                        first = False
            for s in range(GROUP):
                t = g * GROUP + s
                tile = pltpu.matmul_pop(accs[unit][0][t])
                dest = jnp.where(t < live, codes[t] % dest_rows, dest_rows)
                total[dest] = total[dest] + tile

    def per_disp(ll, carry):
        pltpu.make_async_copy(wbuf.at[ll], wbuf.at[ll], sems.at[ll]).wait()
        start, stop = offs[ll], offs[ll + 1]

        def per_block(blk, inner):
            base = start + blk * BLOCK
            live = jnp.minimum(stop - base, BLOCK)
            lax.switch(
                (live + GROUP - 1) // GROUP - 1,
                [functools.partial(block_body, ll, base, live, GROUP * (c + 1)) for c in range(BLOCK // GROUP)],
            )
            return inner

        lax.fori_loop(0, (stop - start + BLOCK - 1) // BLOCK, per_block, 0)
        return carry

    lax.fori_loop(0, disp_count, per_disp, 0)
    for r, out_ref in enumerate(out_refs):
        out_ref[...] = total[pl.ds(r * block_boxes, block_boxes)].astype(jnp.bfloat16)


SMEM = pl.BlockSpec(memory_space=pltpu.SMEM)
VMEM = pl.BlockSpec(memory_space=pltpu.VMEM)
ANY = pl.BlockSpec(memory_space=pl.ANY)


def convolve(sources, shifted, yz_kernels, packed, offs, dest_count, term_count, order_k):
    plane = order_k * order_k
    block_boxes = sources[0].shape[0]
    disp_count = yz_kernels.shape[1] // (term_count * plane)
    dims = (term_count, order_k, disp_count, len(sources), dest_count)
    tile = jax.ShapeDtypeStruct((block_boxes, order_k, plane), jnp.bfloat16)
    return pl.pallas_call(
        functools.partial(conv_kernel, dims),
        out_shape=[tile] * dest_count,
        in_specs=[SMEM, SMEM] + [ANY] * len(sources) + [VMEM, ANY],
        out_specs=[VMEM] * dest_count,
        scratch_shapes=[
            pltpu.VMEM((disp_count, term_count, plane, plane), jnp.bfloat16),
            pltpu.VMEM((BLOCK * term_count * order_k, plane), jnp.bfloat16),
            pltpu.VMEM((dest_count * block_boxes + 1, order_k, plane), jnp.float32),
            pltpu.VMEM((len(sources) * block_boxes, order_k, plane), jnp.bfloat16),
            pltpu.SemaphoreType.DMA((disp_count,)),
            pltpu.SemaphoreType.DMA((len(sources),)),
        ],
        compiler_params=pltpu.CompilerParams(vmem_limit_bytes=52 * MIB),
        name="convolve",
    )(packed, offs, *sources, shifted, yz_kernels)


def shifted_factors(x_kernels):
    term_count, stacked, order_k = x_kernels.shape
    plane = order_k * order_k
    depth = term_count * order_k
    flat = x_kernels.reshape(term_count, 3, order_k, order_k).transpose(1, 2, 0, 3).reshape(3, order_k, depth)
    padded = jnp.pad(flat, ((0, 0), (0, 0), (plane, plane)))
    parts = {}
    for q in range(GROUP * depth // plane):
        for s in range(GROUP):
            if s * depth < (q + 1) * plane and (s + 1) * depth > q * plane:
                low = plane + q * plane - s * depth
                parts[q + s] = padded[:, :, low : low + plane]
    return jnp.stack([parts[p] for p in range(len(parts))], axis=1)


def route(tables, places, box_ids, here, sizes, disp_rows):
    oct_here, hi_here, lo_here = here
    hi_count, lo_count, block_boxes = sizes
    entries = jnp.take(tables, box_ids, axis=0).reshape(-1)
    slot_count = entries.shape[0]
    live = entries >= 0
    dest = jnp.maximum(entries, 0) // 32
    disp = jnp.maximum(entries, 0) % 32
    box_range = jnp.arange(places.shape[0], dtype=jnp.int32)
    place = jnp.sum(jnp.where(dest[:, None] == box_range[None, :], places[None, :], 0), axis=1)
    owner = place // block_boxes
    keep = live & (owner // (hi_count * lo_count) == oct_here) & (owner % lo_count == lo_here)
    away = ((owner // lo_count) % hi_count) ^ hi_here
    row = disp % disp_rows
    key = jnp.where(keep, row, disp_rows)
    index = jnp.arange(slot_count, dtype=jnp.int32)
    full_key = key * slot_count + index
    position = jnp.sum((full_key[None, :] < full_key[:, None]).astype(jnp.int32), axis=1)
    source = index // (slot_count // box_ids.shape[0])
    code = (source * 4 + disp // disp_rows) * (hi_count * block_boxes) + away * block_boxes + place % block_boxes
    listed = jnp.arange(slot_count + BLOCK, dtype=jnp.int32)
    packed = jnp.sum(jnp.where(position[None, :] == listed[:, None], code[None, :], 0), axis=1)
    bounds = jnp.arange(16, dtype=jnp.int32)
    offs = jnp.sum((key[None, :] < bounds[:, None]).astype(jnp.int32), axis=1)
    return packed, offs


def flips(count, step):
    return [(i, i ^ step) for i in range(count)]


def gather_sources(source, lo_count):
    near = [source] + [lax.ppermute(source, "lo", flips(lo_count, r)) for r in range(1, lo_count)]
    return near + [lax.ppermute(block, "oct", flips(2, 1)) for block in near]


def shards(
    coefficients,
    potential,
    to_values,
    x_kernels,
    yz_kernels,
    two_scale,
    disp_ids,
    dest_box,
    parent_of,
    child_octant,
):
    box_count, slot_count = disp_ids.shape
    order_k = to_values.shape[0]
    plane = order_k * order_k
    term_count = x_kernels.shape[0]
    disp_rows = yz_kernels.shape[1] // (term_count * plane)
    oct_count, hi_count, lo_count = (lax.axis_size(name) for name in ("oct", "hi", "lo"))
    here = tuple(lax.axis_index(name) for name in ("oct", "hi", "lo"))
    oct_here, hi_here, lo_here = here
    sub_count = hi_count * lo_count
    devices_all = oct_count * sub_count
    sub_here = hi_here * lo_count + lo_here
    sizes = (hi_count, lo_count, box_count)
    flipped = jnp.swapaxes(two_scale, 1, 2)
    back_values = to_values.T

    own_place = parent_of * 8 + child_octant
    own_owner = own_place // box_count - oct_here * sub_count
    own_table = jnp.where(dest_box >= 0, dest_box * 32 + disp_ids, -1)
    words = jnp.concatenate([own_table.reshape(-1), own_place])
    words = jnp.pad(words, (0, -words.shape[0] % 1024)).reshape(-1, 128)
    words = lax.all_to_all(
        jnp.broadcast_to(words[None], (devices_all,) + words.shape), ("oct", "hi", "lo"), 0, 0, tiled=True
    ).reshape(devices_all, -1)
    tables = words[:, : box_count * slot_count].reshape(devices_all * box_count, slot_count)
    places = words[:, box_count * slot_count : box_count * (slot_count + 1)].reshape(-1)

    source = pl.pallas_call(
        first_kernel,
        out_shape=jax.ShapeDtypeStruct((box_count, order_k, plane), jnp.bfloat16),
        in_specs=[VMEM] * 4,
        out_specs=VMEM,
        name="first_source",
    )(coefficients, potential, to_values, back_values)

    group_devices = jnp.stack(
        [
            (oct_here ^ (r // lo_count)) * sub_count + hi_here * lo_count + (lo_here ^ (r % lo_count))
            for r in range(2 * lo_count)
        ]
    )
    group_rows = (group_devices[:, None] * box_count + jnp.arange(box_count)[None, :]).reshape(-1)
    all_rows = jnp.arange(devices_all * box_count, dtype=jnp.int32)
    moved_rows = jnp.sum(
        jnp.where(places[None, :] == group_rows[:, None], all_rows[None, :], 0), axis=1
    )
    shifted = shifted_factors(x_kernels)

    peers = jnp.arange(sub_count, dtype=jnp.int32)
    send_hit = own_owner[None, :] == peers[:, None]
    send_row = jnp.sum(jnp.where(send_hit, jnp.arange(box_count)[None, :], 0), axis=1)
    moved_own = lax.dynamic_slice_in_dim(moved_rows, 0, box_count)
    came_from = moved_own // box_count - oct_here * sub_count
    pick_hit = came_from[None, :] == peers[:, None]
    pick = jnp.sum(jnp.where(pick_hit, jnp.arange(box_count)[None, :], 0), axis=1)

    moved_potential = lax.all_to_all(
        jnp.take(potential.reshape(box_count, order_k, plane), send_row, axis=0),
        ("hi", "lo"),
        0,
        0,
        tiled=True,
    )
    moved_potential = jnp.take(moved_potential, came_from, axis=0)

    tile = (box_count, order_k, plane)
    for iteration in range(ITERS):
        last = iteration == ITERS - 1
        sources = gather_sources(source, lo_count)
        rows = group_rows if iteration == 0 else moved_rows
        packed, offs = route(tables, places, rows, here, sizes, disp_rows)
        outs = convolve(sources, shifted, yz_kernels, packed, offs, hi_count, term_count, order_k)
        parts = [outs[0]] + [lax.ppermute(outs[r], "hi", flips(hi_count, r)) for r in range(1, hi_count)]
        kernel = functools.partial(tree_kernel, last, hi_count)
        if last:
            fields, parents = pl.pallas_call(
                kernel,
                out_shape=[
                    jax.ShapeDtypeStruct((sub_count, order_k, plane), jnp.float32),
                    jax.ShapeDtypeStruct((box_count // 8, order_k * plane), jnp.float32),
                ],
                in_specs=[VMEM] * (hi_count + 2) + [SMEM],
                out_specs=[VMEM] * 2,
                scratch_shapes=[pltpu.VMEM(tile, jnp.float32)],
                name="last_tree",
            )(*parts, two_scale, flipped, pick)
        else:
            source = pl.pallas_call(
                kernel,
                out_shape=jax.ShapeDtypeStruct(tile, jnp.bfloat16),
                in_specs=[VMEM] * (hi_count + 5),
                out_specs=VMEM,
                name="tree_source",
            )(*parts, two_scale, flipped, moved_potential, to_values, back_values)
    returned = lax.all_to_all(fields, ("hi", "lo"), 0, 0, tiled=True)
    next_field = jnp.take(returned, own_owner, axis=0).reshape(box_count, order_k * plane)
    return next_field, parents


def solution(mesh):
    oct_count, sub_count = mesh.devices.shape
    lo_count = 4
    split = Mesh(mesh.devices.reshape(oct_count, sub_count // lo_count, lo_count), ("oct", "hi", "lo"))
    rows = ("oct", "hi", "lo")
    placed = (
        P(rows, None),
        P(rows, None),
        P(),
        P(),
        P(),
        P(),
        P(rows, None),
        P(rows, None),
        P(rows),
        P(rows),
    )
    return jax.shard_map(
        shards,
        mesh=split,
        in_specs=placed,
        out_specs=(P(rows, None), P(rows, None)),
        check_vma=False,
    )
```

```python
import functools

import jax
import jax.numpy as jnp
from jax import lax
from jax.experimental import pallas as pl
from jax.experimental.pallas import tpu as pltpu
from jax.sharding import Mesh
from jax.sharding import PartitionSpec as P

ITERS = 2
BLOCK = 32
GROUP = 4
LANES = 128
MIB = 1024 * 1024
SMEM = pl.BlockSpec(memory_space=pltpu.SMEM)
VMEM = pl.BlockSpec(memory_space=pltpu.VMEM)
ANY = pl.BlockSpec(memory_space=pl.ANY)


def iota(shape, dim):
    return lax.broadcasted_iota(jnp.int32, shape, dim)


def mm(left, right):
    return jnp.dot(left, right, precision=lax.Precision.HIGHEST, preferred_element_type=jnp.float32)


def dot16(left, right):
    return jnp.dot(left, right, preferred_element_type=jnp.float32)


def halves(matrix):
    high = matrix.astype(jnp.bfloat16)
    return high, (matrix - high.astype(jnp.float32)).astype(jnp.bfloat16)


def mm_halves(left, right):
    rows = left[0].shape[0]
    both = dot16(jnp.concatenate(left, axis=0), right[0])
    return both[:rows] + both[rows:] + dot16(left[0], right[1])


def rows_high(matrix):
    order_k, width = matrix.shape
    return jnp.broadcast_to(matrix[:, None, :], (order_k, order_k, width)).reshape(order_k * order_k, width)


def rows_low(matrix):
    order_k, width = matrix.shape
    return jnp.broadcast_to(matrix[None, :, :], (order_k, order_k, width)).reshape(order_k * order_k, width)


def spread_columns(matrix):
    order_k = matrix.shape[0]
    shape = (order_k, order_k * order_k)
    slot, lane = iota(shape, 0), iota(shape, 1)
    high = (lane // order_k == slot).astype(jnp.float32)
    low = (lane % order_k == slot).astype(jnp.float32)
    return mm(matrix, high), mm(matrix, low)


def masks(order_k):
    shape = (order_k * order_k, order_k * order_k)
    row, lane = iota(shape, 0), iota(shape, 1)
    return row // order_k, row % order_k, lane // order_k, lane % order_k


def pack_kernel(info, disp_ref, dest_ref, place_ref, out_ref):
    boxes, slots = disp_ref.shape
    half = boxes // 2
    dest = dest_ref[...]
    entry = jnp.where(dest >= 0, dest * 32 + disp_ref[...] + 1, 0).astype(jnp.float32)
    lane = iota((slots, LANES), 1)
    slot = iota((slots, LANES), 0)
    lane_out = iota((half, LANES), 1)
    row_out = iota((half, LANES), 0)
    words = jnp.zeros((half, LANES), jnp.float32)
    for h in range(2):
        start = h * (LANES // 2)
        words += mm(entry[h * half : (h + 1) * half], (lane == slot + start).astype(jnp.float32))
    words = words.astype(jnp.int32)
    for h in range(2):
        start = h * (LANES // 2)
        place = place_ref[h * half : (h + 1) * half, :]
        words = jnp.where(lane_out == start + slots, place, words)
        words = jnp.where(lane_out == start + slots + 1, info[3] * boxes + h * half + row_out, words)
    for d in range(out_ref.shape[0]):
        out_ref[d] = words


def first_kernel(coef_ref, pot_ref, to_ref, back_ref, out_ref):
    order_k = to_ref.shape[0]
    plane = order_k * order_k
    to_high, to_low = spread_columns(to_ref[...])
    back_high, back_low = spread_columns(back_ref[...])
    row_high, row_low, lane_high, lane_low = masks(order_k)
    value_pair = halves(rows_high(back_high) * rows_low(back_low))
    back_pair = halves(rows_high(to_high) * rows_low(to_low))
    value_x = halves(jnp.where(row_low == lane_low, rows_high(to_high), 0.0))
    source_x = halves(jnp.where(row_high == lane_low, rows_low(back_high), 0.0))

    def by_x(ref):
        return jnp.concatenate([ref[:, x * plane : (x + 1) * plane] for x in range(order_k)], axis=0)

    values = mm_halves(value_x, halves(mm_halves(halves(by_x(coef_ref)), value_pair)))
    product = values * (by_x(pot_ref) + 0.25 * values * values)
    source = mm_halves(source_x, halves(mm_halves(halves(product), back_pair)))
    out_ref[...] = source.astype(jnp.bfloat16).reshape(out_ref.shape)


def route_kernel(dims, info, words_ref, w_hbm, *refs):
    oct_count, hi_count, lo_count, boxes, slots, disp_rows = dims
    list_refs, moved_ref, held_ref, sem = refs[:ITERS], refs[ITERS], refs[ITERS + 1], refs[ITERS + 2]
    load = pltpu.make_async_copy(w_hbm, held_ref, sem)
    load.start()
    oct_here, hi_here, lo_here = info[0], info[1], info[2]
    width = LANES // 2
    words = words_ref[...].reshape(-1, LANES)
    table = jnp.concatenate([words[:, :width], words[:, width:]], axis=0)
    total = table.shape[0]
    place_col, id_col = table[:, slots : slots + 1], table[:, slots + 1 : slots + 2]
    flat = table.astype(jnp.float32).T.astype(jnp.int32)
    low = (flat % 256).astype(jnp.float32).astype(jnp.bfloat16)
    high = (flat // 256).astype(jnp.float32).astype(jnp.bfloat16)

    def look(hit):
        chosen = hit.astype(jnp.float32).astype(jnp.bfloat16)
        return (dot16(low, chosen) + 256.0 * dot16(high, chosen)).astype(jnp.int32)

    lanes = oct_count * lo_count * boxes
    lane = iota((1, lanes), 1)
    member = lane // boxes
    device = ((member // lo_count) ^ oct_here) * (hi_count * lo_count) + hi_here * lo_count
    device = device + ((member % lo_count) ^ lo_here)
    target = device * boxes + lane % boxes
    dest_rows = hi_count * boxes
    source = iota((slots, lanes), 1)
    list_rows = list_refs[0].shape[0]
    upper = (iota((lanes, lanes), 0) < iota((lanes, lanes), 1)).astype(jnp.float32).astype(jnp.bfloat16)
    ones = jnp.ones((lanes, lanes), jnp.bfloat16)
    ranks = disp_rows * slots
    lower = (iota((ranks, ranks), 1) < iota((ranks, ranks), 0)).astype(jnp.float32).astype(jnp.bfloat16)
    for it in range(ITERS):
        found = look((id_col if it == 0 else place_col) == target)
        if it == 1:
            moved_ref[...] = found[slots : slots + 8]
        entry = found[:slots] - 1
        dest = jnp.where(entry >= 0, entry // 32, -1)
        disp = jnp.maximum(entry, 0) % 32
        place = jnp.concatenate(
            [look(id_col == dest[s : s + 1])[slots : slots + 1] for s in range(slots)], axis=0
        )
        owner = place // boxes
        keep = (entry >= 0) & (owner // (hi_count * lo_count) == oct_here) & (owner % lo_count == lo_here)
        away = ((owner // lo_count) % hi_count) ^ hi_here
        shift = jnp.zeros_like(disp)
        for c in range(1, 3):
            shift += (disp >= c * disp_rows).astype(jnp.int32)
        row = disp - shift * disp_rows
        member_of = [keep & (row == g) for g in range(disp_rows)]
        marks = jnp.concatenate(member_of, axis=0).astype(jnp.float32).astype(jnp.bfloat16)
        sums = dot16(marks, ones)
        starts = dot16(lower, sums.astype(jnp.bfloat16))
        ordinal = (starts + dot16(marks, upper)).astype(jnp.int32)
        position = jnp.full((slots, lanes), -1, jnp.int32)
        for g in range(disp_rows):
            position = jnp.where(member_of[g], ordinal[g * slots : (g + 1) * slots], position)
        code = (source * 4 + shift) * dest_rows + away * boxes + place % boxes
        pieces = [((code // 256**n) % 256).astype(jnp.float32) for n in range(3)]
        listed = jnp.zeros((3 * list_rows, LANES), jnp.float32)
        for s in range(slots):
            spot = position[s : s + 1]
            in_row = (spot // LANES == iota((list_rows, lanes), 0)) & (spot >= 0)
            left = jnp.concatenate([jnp.where(in_row, piece[s : s + 1], 0.0) for piece in pieces], axis=0)
            in_lane = (spot % LANES == iota((LANES, lanes), 0)).astype(jnp.float32).astype(jnp.bfloat16)
            listed += lax.dot_general(
                left.astype(jnp.bfloat16), in_lane, (((1,), (1,)), ((), ())), preferred_element_type=jnp.float32
            )
        packed = sum(
            listed[n * list_rows : (n + 1) * list_rows].astype(jnp.int32) * 256**n for n in range(3)
        )
        bound = (starts[ranks - 1 : ranks] + sums[ranks - 1 : ranks]).astype(jnp.int32)
        for g in range(disp_rows):
            bound = jnp.where(lane == g, starts[g * slots : g * slots + 1].astype(jnp.int32), bound)
        list_refs[it][...] = jnp.where(iota(packed.shape, 0) == list_rows - 7, bound, packed)
    load.wait()


def constants_kernel(owner, pot_ref, to_ref, back_ref, two_ref, flip_ref, mats_ref, lift_ref, drop_ref, pot_out, rows_ref):
    order_k = to_ref.shape[0]
    plane = order_k * order_k
    to_high, to_low = spread_columns(to_ref[...])
    back_high, back_low = spread_columns(back_ref[...])
    two = [spread_columns(two_ref[c]) for c in range(2)]
    flip = [spread_columns(flip_ref[c]) for c in range(2)]
    row_high, row_low, lane_high, lane_low = masks(order_k)
    made = []
    for quad in range(4):
        made.append(rows_high(flip[quad // 2][0]) * rows_low(flip[quad % 2][1]))
    for quad in range(4):
        made.append(rows_high(two[quad // 2][0]) * rows_low(two[quad % 2][1]))
    made.append(rows_high(back_high) * rows_low(back_low))
    made.append(rows_high(to_high) * rows_low(to_low))
    made.append(jnp.where(row_high == lane_high, rows_low(to_low), 0.0))
    made.append(jnp.where(row_high == lane_high, rows_low(back_low), 0.0))
    for n, matrix in enumerate(made):
        mats_ref[n, 0], mats_ref[n, 1] = halves(matrix)
    parents, wide = lift_ref.shape
    shape = (order_k, wide)
    lifted = jnp.zeros(shape, jnp.float32)
    for c in range(2):
        hot = (iota(shape, 1) % order_k == iota(shape, 0)) & ((iota(shape, 1) // order_k) % 2 == c)
        lifted += mm(two_ref[c], hot.astype(jnp.float32))
    lifted = jnp.concatenate([lifted] * (parents // order_k), axis=0)
    lift_ref[...] = jnp.where(
        iota(lift_ref.shape, 0) // order_k == iota(lift_ref.shape, 1) // (2 * order_k), lifted, 0.0
    )
    hot = (iota((order_k, parents), 1) % order_k == iota((order_k, parents), 0)).astype(jnp.float32)
    dropped = jnp.concatenate([mm(flip_ref[c], hot) for c in range(2)] * (parents // order_k), axis=0)
    drop_ref[...] = jnp.where(
        iota(drop_ref.shape, 0) // (2 * order_k) == iota(drop_ref.shape, 1) // order_k, dropped, 0.0
    )
    if rows_ref.shape[0] > pot_ref.shape[0]:
        rows_ref[...] = jnp.zeros_like(rows_ref)
    for b in range(pot_ref.shape[0]):
        peer = owner[b]
        for x in range(order_k):
            rows_ref[peer, x : x + 1, :] = pot_ref[b : b + 1, x * plane : (x + 1) * plane]
    pot_out[...] = rows_ref[...].astype(jnp.bfloat16)


def tree_kernel(last, part_count, came_from, *refs):
    parts = refs[:part_count]
    mats_ref, lift_ref, drop_ref = refs[part_count : part_count + 3]
    rest = refs[part_count + 3 :]
    gathered = parts[0][...].astype(jnp.float32)
    for part in parts[1:]:
        gathered = gathered + part[...].astype(jnp.float32)
    boxes, order_k, plane = gathered.shape
    parent_count = boxes // 8

    def matrix(n):
        return mats_ref[n, 0], mats_ref[n, 1]

    summed = None
    for quad in range(4):
        stacked = jnp.concatenate(
            [gathered[8 * p + 4 * c + quad] for p in range(parent_count) for c in range(2)], axis=0
        )
        inner = mm_halves(halves(stacked), matrix(quad))
        summed = inner if summed is None else summed + inner
    own = mm_halves(halves(lift_ref[...]), halves(summed))
    dropped_x = halves(mm_halves(halves(drop_ref[...]), halves(own)))
    dropped = [mm_halves(dropped_x, matrix(4 + quad)) for quad in range(4)]
    fields = []
    for b in range(boxes):
        start = (b // 4) * order_k
        fields.append(gathered[b] - dropped[b % 4][start : start + order_k])
    if last:
        field_ref, parent_ref = rest
        if field_ref.shape[0] > boxes:
            field_ref[...] = jnp.zeros_like(field_ref)
        for b in range(boxes):
            field_ref[came_from[b]] = fields[b].astype(field_ref.dtype)
        for p in range(parent_count):
            for i in range(order_k):
                parent_ref[p : p + 1, i * plane : (i + 1) * plane] = own[p * order_k + i : p * order_k + i + 1]
    else:
        pot_ref, out_ref = rest
        potential = jnp.concatenate([pot_ref[came_from[b]] for b in range(boxes)], axis=0).astype(jnp.float32)
        current = halves(jnp.concatenate(fields, axis=0))
        values = mm_halves(matrix(10), halves(mm_halves(current, matrix(8))))
        product = values * (potential + 0.25 * values * values)
        source = mm_halves(matrix(11), halves(mm_halves(halves(product), matrix(9))))
        out_ref[...] = source.astype(jnp.bfloat16).reshape(out_ref.shape)


def unpack_kernel(owner, field_ref, out_ref):
    order_k, plane = field_ref.shape[1:]
    for b in range(out_ref.shape[0]):
        box = field_ref[owner[b]].astype(jnp.float32)
        for x in range(order_k):
            out_ref[b : b + 1, x * plane : (x + 1) * plane] = box[x : x + 1]


def conv_kernel(dims, packed, *refs):
    term_count, order_k, disp_count, source_count, dest_count = dims
    source_refs = refs[:source_count]
    xl_ref, w_ref = refs[source_count : source_count + 2]
    out_refs = refs[source_count + 2 : source_count + 2 + dest_count]
    pbuf, total, held, held_sems = refs[source_count + 2 + dest_count :]
    plane = order_k * order_k
    list_rows = packed.shape[0] - 7
    half = term_count // 2
    depth = term_count * order_k
    block_boxes = out_refs[0].shape[0]
    dest_rows = dest_count * block_boxes
    loads = [
        pltpu.make_async_copy(ref, held.at[pl.ds(n * block_boxes, block_boxes)], held_sems.at[n])
        for n, ref in enumerate(source_refs)
    ]
    for load in loads:
        load.start()
    total[...] = jnp.zeros_like(total)
    for load in loads:
        load.wait()

    def push_w(ll, j, reg):
        for unit in range(2):
            column = pl.multiple_of(((unit * half + j) * disp_count + ll) * plane, plane)
            pltpu.matmul_push_rhs(w_ref[:, pl.ds(column, plane)], reg, unit)

    def block_body(ll, base, live, slots):
        pl.run_scoped(
            functools.partial(with_accs, ll, base, live, slots),
            *[
                [
                    [pltpu.ACC(unit)((order_k, plane), jnp.float32) for _ in range(slots)]
                    for _ in range(max(2, min(half, 2 * BLOCK // slots)))
                ]
                for unit in range(2)
            ],
        )

    def with_accs(ll, base, live, slots, *accs):
        codes = [packed[(base + t) // LANES, (base + t) % LANES] for t in range(slots)]
        ids = [code // (4 * dest_rows) for code in codes]
        shifts = [(code // dest_rows) % 4 for code in codes]

        stages = len(accs[0])

        def take(j, t):
            for unit in range(2):
                row = (unit * half + j) * order_k + t * depth
                tile = pltpu.matmul_pop(accs[unit][j % stages][t])
                pbuf[row : row + order_k, :] = tile.astype(jnp.bfloat16)

        push_w(ll, 0, 0)
        for j in range(half):
            if j + 1 < half:
                push_w(ll, j + 1, (j + 1) % 2)
            for t in range(slots):
                lhs = held[ids[t]]
                for unit in range(2):
                    pltpu.matmul_acc_lhs(accs[unit][j % stages][t], lhs, j % 2 if t == 0 else None)
                if j + 1 >= stages:
                    take(j + 1 - stages, t)
        for j in range(half - stages + 1, half):
            for t in range(slots):
                take(j, t)

        tiles = GROUP * depth // plane
        groups = slots // GROUP

        def place(g):
            for s in range(GROUP):
                t = g * GROUP + s
                tile = pltpu.matmul_pop(accs[g % 2][0][t])
                dest = jnp.where(t < live, codes[t] % dest_rows, dest_rows)
                total[dest] = total[dest] + tile

        for g in range(groups):
            unit = g % 2
            for q in range(tiles):
                reg = q % 2
                pltpu.matmul_push_rhs(pbuf[pl.ds(g * GROUP * depth + q * plane, plane), :], reg, unit)
                first = True
                for s in range(GROUP):
                    if s * depth < (q + 1) * plane and (s + 1) * depth > q * plane:
                        t = g * GROUP + s
                        pltpu.matmul_acc_lhs(
                            accs[unit][0][t], xl_ref[shifts[t], q + s], reg if first else None
                        )
                        first = False
            if g >= 3:
                place(g - 3)
        for g in range(max(groups - 3, 0), groups):
            place(g)

    def per_disp(ll, carry):
        start, stop = packed[list_rows, ll], packed[list_rows, ll + 1]

        def per_block(blk, inner):
            base = start + blk * BLOCK
            live = jnp.minimum(stop - base, BLOCK)
            lax.switch(
                (live + GROUP - 1) // GROUP - 1,
                [functools.partial(block_body, ll, base, live, GROUP * (c + 1)) for c in range(BLOCK // GROUP)],
            )
            return inner

        lax.fori_loop(0, (stop - start + BLOCK - 1) // BLOCK, per_block, 0)
        return carry

    lax.fori_loop(0, disp_count, per_disp, 0)
    for r, out_ref in enumerate(out_refs):
        out_ref[...] = total[pl.ds(r * block_boxes, block_boxes)].astype(jnp.bfloat16)


def shifted_factors(x_kernels):
    term_count, stacked, order_k = x_kernels.shape
    plane = order_k * order_k
    depth = term_count * order_k
    flat = x_kernels.reshape(term_count, 3, order_k, order_k).transpose(1, 2, 0, 3).reshape(3, order_k, depth)
    padded = jnp.pad(flat, ((0, 0), (0, 0), (plane, plane)))
    parts = {}
    for q in range(GROUP * depth // plane):
        for s in range(GROUP):
            if s * depth < (q + 1) * plane and (s + 1) * depth > q * plane:
                low = plane + q * plane - s * depth
                parts[q + s] = padded[:, :, low : low + plane]
    return jnp.stack([parts[p] for p in range(len(parts))], axis=1)


def convolve(sources, shifted, held_kernels, packed, dest_count, term_count, order_k):
    plane = order_k * order_k
    block_boxes = sources[0].shape[0]
    disp_count = held_kernels.shape[1] // (term_count * plane)
    dims = (term_count, order_k, disp_count, len(sources), dest_count)
    tile = jax.ShapeDtypeStruct((block_boxes, order_k, plane), jnp.bfloat16)
    return pl.pallas_call(
        functools.partial(conv_kernel, dims),
        out_shape=[tile] * dest_count,
        in_specs=[SMEM] + [ANY] * len(sources) + [VMEM, VMEM],
        out_specs=[VMEM] * dest_count,
        scratch_shapes=[
            pltpu.VMEM((BLOCK * term_count * order_k, plane), jnp.bfloat16),
            pltpu.VMEM((dest_count * block_boxes + 1, order_k, plane), jnp.float32),
            pltpu.VMEM((len(sources) * block_boxes, order_k, plane), jnp.bfloat16),
            pltpu.SemaphoreType.DMA((len(sources),)),
        ],
        compiler_params=pltpu.CompilerParams(vmem_limit_bytes=20 * MIB),
        name="convolve",
    )(packed, *sources, shifted, held_kernels)


def flips(count, step):
    return [(i, i ^ step) for i in range(count)]


def gather_sources(source, lo_count):
    near = [source] + [lax.ppermute(source, "lo", flips(lo_count, r)) for r in range(1, lo_count)]
    return near + [lax.ppermute(block, "oct", flips(2, 1)) for block in near]


def shards(
    coefficients,
    potential,
    to_values,
    x_kernels,
    yz_kernels,
    two_scale,
    disp_ids,
    dest_box,
    parent_of,
    child_octant,
):
    box_count, slot_count = disp_ids.shape
    order_k = to_values.shape[0]
    plane = order_k * order_k
    term_count = x_kernels.shape[0]
    disp_rows = yz_kernels.shape[1] // (term_count * plane)
    oct_count, hi_count, lo_count = (lax.axis_size(name) for name in ("oct", "hi", "lo"))
    oct_here, hi_here, lo_here = (lax.axis_index(name) for name in ("oct", "hi", "lo"))
    sub_count = hi_count * lo_count
    devices_all = oct_count * sub_count
    device_here = oct_here * sub_count + hi_here * lo_count + lo_here
    info = jnp.stack([oct_here, hi_here, lo_here, device_here]).astype(jnp.int32)
    flipped = jnp.swapaxes(two_scale, 1, 2)
    back_values = to_values.T
    tile = (box_count, order_k, plane)

    own_place = parent_of * 8 + child_octant
    own_owner = own_place // box_count % sub_count
    words = pl.pallas_call(
        pack_kernel,
        out_shape=jax.ShapeDtypeStruct((devices_all, box_count // 2, LANES), jnp.int32),
        in_specs=[SMEM] + [VMEM] * 3,
        out_specs=VMEM,
        name="pack_tables",
    )(info, disp_ids, dest_box, own_place.reshape(box_count, 1))
    words = lax.all_to_all(words, ("oct", "hi", "lo"), 0, 0, tiled=True)

    source = pl.pallas_call(
        first_kernel,
        out_shape=jax.ShapeDtypeStruct(tile, jnp.bfloat16),
        in_specs=[VMEM] * 4,
        out_specs=VMEM,
        name="first_source",
    )(coefficients, potential, to_values, back_values)

    list_rows = -(-(oct_count * lo_count * box_count * slot_count // LANES + 8) // 8) * 8
    *lists, moved, held_kernels = pl.pallas_call(
        functools.partial(route_kernel, (oct_count, hi_count, lo_count, box_count, slot_count, disp_rows)),
        out_shape=[jax.ShapeDtypeStruct((list_rows, LANES), jnp.int32)] * ITERS
        + [
            jax.ShapeDtypeStruct((8, LANES), jnp.int32),
            pltpu.VMEM(yz_kernels.shape, yz_kernels.dtype),
        ],
        in_specs=[SMEM, VMEM, ANY],
        out_specs=[VMEM] * (ITERS + 2),
        scratch_shapes=[pltpu.SemaphoreType.DMA],
        compiler_params=pltpu.CompilerParams(vmem_limit_bytes=20 * MIB),
        name="route_slots",
    )(info, words, yz_kernels)
    came_from = moved[1, :box_count] // box_count % sub_count
    shifted = shifted_factors(x_kernels)

    for iteration in range(ITERS):
        last = iteration == ITERS - 1
        sources = gather_sources(source, lo_count)
        outs = convolve(sources, shifted, held_kernels, lists[iteration], hi_count, term_count, order_k)
        if not last:
            late, outs = lax.optimization_barrier(((potential, own_owner), outs))
            parents = box_count // 8 * order_k
            *fixed, send_potential = pl.pallas_call(
                constants_kernel,
                out_shape=[
                    jax.ShapeDtypeStruct((12, 2, plane, plane), jnp.bfloat16),
                    jax.ShapeDtypeStruct((parents, 2 * parents), jnp.float32),
                    jax.ShapeDtypeStruct((2 * parents, parents), jnp.float32),
                    jax.ShapeDtypeStruct((sub_count, order_k, plane), jnp.bfloat16),
                ],
                in_specs=[SMEM] + [VMEM] * 5,
                out_specs=[VMEM] * 4,
                scratch_shapes=[pltpu.VMEM((sub_count, order_k, plane), jnp.float32)],
                compiler_params=pltpu.CompilerParams(vmem_limit_bytes=16 * MIB),
                name="make_constants",
            )(late[1], late[0], to_values, back_values, two_scale, flipped)
        parts = [outs[0]] + [lax.ppermute(outs[r], "hi", flips(hi_count, r)) for r in range(1, hi_count)]
        kernel = functools.partial(tree_kernel, last, hi_count)
        if last:
            fields, parents = pl.pallas_call(
                kernel,
                out_shape=[
                    jax.ShapeDtypeStruct((sub_count, order_k, plane), jnp.bfloat16),
                    jax.ShapeDtypeStruct((box_count // 8, order_k * plane), jnp.float32),
                ],
                in_specs=[SMEM] + [VMEM] * (hi_count + 3),
                out_specs=[VMEM] * 2,
                name="last_tree",
            )(came_from, *parts, *fixed)
        else:
            moved_potential = lax.all_to_all(send_potential, ("hi", "lo"), 0, 0, tiled=True)
            source = pl.pallas_call(
                kernel,
                out_shape=jax.ShapeDtypeStruct(tile, jnp.bfloat16),
                in_specs=[SMEM] + [VMEM] * (hi_count + 4),
                out_specs=VMEM,
                name="tree_source",
            )(came_from, *parts, *fixed, moved_potential)
    returned = lax.all_to_all(fields, ("hi", "lo"), 0, 0, tiled=True)
    next_field = pl.pallas_call(
        unpack_kernel,
        out_shape=jax.ShapeDtypeStruct((box_count, order_k * plane), jnp.float32),
        in_specs=[SMEM, VMEM],
        out_specs=VMEM,
        name="unpack_fields",
    )(own_owner, returned)
    return next_field, parents


def solution(mesh):
    oct_count, sub_count = mesh.devices.shape
    lo_count = 4
    split = Mesh(mesh.devices.reshape(oct_count, sub_count // lo_count, lo_count), ("oct", "hi", "lo"))
    rows = ("oct", "hi", "lo")
    placed = (
        P(rows, None),
        P(rows, None),
        P(),
        P(),
        P(),
        P(),
        P(rows, None),
        P(rows, None),
        P(rows),
        P(rows),
    )
    return jax.shard_map(
        shards,
        mesh=split,
        in_specs=placed,
        out_specs=(P(rows, None), P(rows, None)),
        check_vma=False,
    )
```

```python
import functools

import jax
import jax.numpy as jnp
from jax import lax
from jax.experimental import pallas as pl
from jax.experimental.pallas import tpu as pltpu
from jax.sharding import Mesh
from jax.sharding import PartitionSpec as P

ITERS = 2
BLOCK = 32
GROUP = 4
LANES = 128
MIB = 1024 * 1024
SMEM = pl.BlockSpec(memory_space=pltpu.SMEM)
VMEM = pl.BlockSpec(memory_space=pltpu.VMEM)
ANY = pl.BlockSpec(memory_space=pl.ANY)


def iota(shape, dim):
    return lax.broadcasted_iota(jnp.int32, shape, dim)


def mm(left, right):
    return jnp.dot(left, right, precision=lax.Precision.HIGHEST, preferred_element_type=jnp.float32)


def dot16(left, right):
    return jnp.dot(left, right, preferred_element_type=jnp.float32)


def halves(matrix):
    high = matrix.astype(jnp.bfloat16)
    return high, (matrix - high.astype(jnp.float32)).astype(jnp.bfloat16)


def mm_halves(left, right):
    rows = left[0].shape[0]
    both = dot16(jnp.concatenate(left, axis=0), right[0])
    return both[:rows] + both[rows:] + dot16(left[0], right[1])


def rows_high(matrix):
    order_k, width = matrix.shape
    return jnp.broadcast_to(matrix[:, None, :], (order_k, order_k, width)).reshape(order_k * order_k, width)


def rows_low(matrix):
    order_k, width = matrix.shape
    return jnp.broadcast_to(matrix[None, :, :], (order_k, order_k, width)).reshape(order_k * order_k, width)


def spread_columns(matrix, flip=False):
    order_k = matrix.shape[0]
    shape = (order_k, order_k * order_k)
    slot, lane = iota(shape, 0), iota(shape, 1)
    high = (lane // order_k == slot).astype(jnp.float32)
    low = (lane % order_k == slot).astype(jnp.float32)
    if flip:
        matrix = matrix.T
    return mm(matrix, high), mm(matrix, low)


def masks(order_k):
    shape = (order_k * order_k, order_k * order_k)
    row, lane = iota(shape, 0), iota(shape, 1)
    return row // order_k, row % order_k, lane // order_k, lane % order_k


def pack_kernel(parent_of, octant, disp_ref, dest_ref, out_ref):
    boxes, slots = disp_ref.shape
    half = boxes // 2
    dest = dest_ref[...]
    entry = jnp.where(dest >= 0, dest * 32 + disp_ref[...] + 1, 0).astype(jnp.float32)
    lane = iota((slots, LANES), 1)
    slot = iota((slots, LANES), 0)
    lane_out = iota((half, LANES), 1)
    row_out = iota((half, LANES), 0)
    words = jnp.zeros((half, LANES), jnp.float32)
    for h in range(2):
        start = h * (LANES // 2)
        words += mm(entry[h * half : (h + 1) * half], (lane == slot + start).astype(jnp.float32))
    words = words.astype(jnp.int32)
    for b in range(boxes):
        here = (row_out == b % half) & (lane_out == b // half * (LANES // 2) + slots)
        words = jnp.where(here, parent_of[b] * 8 + octant[b], words)
    for d in range(out_ref.shape[0]):
        out_ref[d] = words


def first_kernel(parent_of, coef_ref, pot_ref, to_ref, out_ref, pot_out, rows_ref):
    order_k = to_ref.shape[0]
    plane = order_k * order_k
    to_high, to_low = spread_columns(to_ref[...])
    back_high, back_low = spread_columns(to_ref[...], True)
    row_high, row_low, lane_high, lane_low = masks(order_k)
    value_pair = halves(rows_high(back_high) * rows_low(back_low))
    back_pair = halves(rows_high(to_high) * rows_low(to_low))
    value_x = halves(jnp.where(row_low == lane_low, rows_high(to_high), 0.0))
    source_x = halves(jnp.where(row_high == lane_low, rows_low(back_high), 0.0))

    def by_x(ref):
        return jnp.concatenate([ref[:, x * plane : (x + 1) * plane] for x in range(order_k)], axis=0)

    values = mm_halves(value_x, halves(mm_halves(halves(by_x(coef_ref)), value_pair)))
    product = values * (by_x(pot_ref) + 0.25 * values * values)
    source = mm_halves(source_x, halves(mm_halves(halves(product), back_pair)))
    out_ref[...] = source.astype(jnp.bfloat16).reshape(out_ref.shape)
    peers = rows_ref.shape[0]
    if peers > pot_ref.shape[0]:
        rows_ref[...] = jnp.zeros_like(rows_ref)
    for b in range(pot_ref.shape[0]):
        peer = parent_of[b] * 8 // pot_ref.shape[0] % peers
        for x in range(order_k):
            rows_ref[peer, x : x + 1, :] = pot_ref[b : b + 1, x * plane : (x + 1) * plane]
    pot_out[...] = rows_ref[...].astype(jnp.bfloat16)


def route_kernel(dims, info, words_ref, w_hbm, *refs):
    oct_count, hi_count, lo_count, boxes, slots, disp_rows = dims
    list_refs, moved_ref, held_ref, sem = refs[:ITERS], refs[ITERS], refs[ITERS + 1], refs[ITERS + 2]
    load = pltpu.make_async_copy(w_hbm, held_ref, sem)
    load.start()
    oct_here, hi_here, lo_here = info[0], info[1], info[2]
    width = LANES // 2
    words = words_ref[...].reshape(-1, LANES)
    table = jnp.concatenate([words[:, :width], words[:, width:]], axis=0)
    total = table.shape[0]

    def box_id(row):
        member = row % (total // 2)
        return member // (boxes // 2) * boxes + row // (total // 2) * (boxes // 2) + member % (boxes // 2)

    place_col, id_col = table[:, slots : slots + 1], box_id(iota((total, 1), 0))
    flat = table.astype(jnp.float32).T.astype(jnp.int32)
    flat = jnp.where(iota(flat.shape, 0) == slots + 1, box_id(iota(flat.shape, 1)), flat)
    low = (flat % 256).astype(jnp.float32).astype(jnp.bfloat16)
    high = (flat // 256).astype(jnp.float32).astype(jnp.bfloat16)

    def look(hit):
        chosen = hit.astype(jnp.float32).astype(jnp.bfloat16)
        return (dot16(low, chosen) + 256.0 * dot16(high, chosen)).astype(jnp.int32)

    lanes = oct_count * lo_count * boxes
    lane = iota((1, lanes), 1)
    member = lane // boxes
    device = ((member // lo_count) ^ oct_here) * (hi_count * lo_count) + hi_here * lo_count
    device = device + ((member % lo_count) ^ lo_here)
    target = device * boxes + lane % boxes
    dest_rows = hi_count * boxes
    source = iota((slots, lanes), 1)
    list_rows = list_refs[0].shape[0]
    upper = (iota((lanes, lanes), 0) < iota((lanes, lanes), 1)).astype(jnp.float32).astype(jnp.bfloat16)
    ones = jnp.ones((lanes, lanes), jnp.bfloat16)
    ranks = disp_rows * slots
    lower = (iota((ranks, ranks), 1) < iota((ranks, ranks), 0)).astype(jnp.float32).astype(jnp.bfloat16)
    for it in range(ITERS):
        found = look((id_col if it == 0 else place_col) == target)
        if it == 1:
            moved_ref[...] = found[slots : slots + 8]
        entry = found[:slots] - 1
        dest = jnp.where(entry >= 0, entry // 32, -1)
        disp = jnp.maximum(entry, 0) % 32
        place = jnp.concatenate(
            [look(id_col == dest[s : s + 1])[slots : slots + 1] for s in range(slots)], axis=0
        )
        owner = place // boxes
        keep = (entry >= 0) & (owner // (hi_count * lo_count) == oct_here) & (owner % lo_count == lo_here)
        away = ((owner // lo_count) % hi_count) ^ hi_here
        shift = jnp.zeros_like(disp)
        for c in range(1, 3):
            shift += (disp >= c * disp_rows).astype(jnp.int32)
        row = disp - shift * disp_rows
        member_of = [keep & (row == g) for g in range(disp_rows)]
        marks = jnp.concatenate(member_of, axis=0).astype(jnp.float32).astype(jnp.bfloat16)
        sums = dot16(marks, ones)
        starts = dot16(lower, sums.astype(jnp.bfloat16))
        ordinal = (starts + dot16(marks, upper)).astype(jnp.int32)
        position = jnp.full((slots, lanes), -1, jnp.int32)
        for g in range(disp_rows):
            position = jnp.where(member_of[g], ordinal[g * slots : (g + 1) * slots], position)
        code = (source * 4 + shift) * dest_rows + away * boxes + place % boxes
        pieces = [((code // 256**n) % 256).astype(jnp.float32) for n in range(3)]
        listed = jnp.zeros((3 * list_rows, LANES), jnp.float32)
        for s in range(slots):
            spot = position[s : s + 1]
            in_row = (spot // LANES == iota((list_rows, lanes), 0)) & (spot >= 0)
            left = jnp.concatenate([jnp.where(in_row, piece[s : s + 1], 0.0) for piece in pieces], axis=0)
            in_lane = (spot % LANES == iota((LANES, lanes), 0)).astype(jnp.float32).astype(jnp.bfloat16)
            listed += lax.dot_general(
                left.astype(jnp.bfloat16), in_lane, (((1,), (1,)), ((), ())), preferred_element_type=jnp.float32
            )
        packed = sum(
            listed[n * list_rows : (n + 1) * list_rows].astype(jnp.int32) * 256**n for n in range(3)
        )
        bound = (starts[ranks - 1 : ranks] + sums[ranks - 1 : ranks]).astype(jnp.int32)
        for g in range(disp_rows):
            bound = jnp.where(lane == g, starts[g * slots : g * slots + 1].astype(jnp.int32), bound)
        list_refs[it][...] = jnp.where(iota(packed.shape, 0) == list_rows - 7, bound, packed)
    load.wait()


def constants_kernel(to_ref, two_ref, mats_ref, lift_ref, drop_ref):
    order_k = to_ref.shape[0]
    to_high, to_low = spread_columns(to_ref[...])
    back_high, back_low = spread_columns(to_ref[...], True)
    two = [spread_columns(two_ref[c]) for c in range(2)]
    flip = [spread_columns(two_ref[c], True) for c in range(2)]
    row_high, row_low, lane_high, lane_low = masks(order_k)
    made = []
    for quad in range(4):
        made.append(rows_high(flip[quad // 2][0]) * rows_low(flip[quad % 2][1]))
    for quad in range(4):
        made.append(rows_high(two[quad // 2][0]) * rows_low(two[quad % 2][1]))
    made.append(rows_high(back_high) * rows_low(back_low))
    made.append(rows_high(to_high) * rows_low(to_low))
    made.append(jnp.where(row_high == lane_high, rows_low(to_low), 0.0))
    made.append(jnp.where(row_high == lane_high, rows_low(back_low), 0.0))
    for n, matrix in enumerate(made):
        mats_ref[n, 0], mats_ref[n, 1] = halves(matrix)
    parents, wide = lift_ref.shape
    shape = (order_k, wide)
    lifted = jnp.zeros(shape, jnp.float32)
    for c in range(2):
        hot = (iota(shape, 1) % order_k == iota(shape, 0)) & ((iota(shape, 1) // order_k) % 2 == c)
        lifted += mm(two_ref[c], hot.astype(jnp.float32))
    lifted = jnp.concatenate([lifted] * (parents // order_k), axis=0)
    lift_ref[...] = jnp.where(
        iota(lift_ref.shape, 0) // order_k == iota(lift_ref.shape, 1) // (2 * order_k), lifted, 0.0
    )
    hot = (iota((order_k, parents), 1) % order_k == iota((order_k, parents), 0)).astype(jnp.float32)
    dropped = jnp.concatenate([mm(two_ref[c].T, hot) for c in range(2)] * (parents // order_k), axis=0)
    drop_ref[...] = jnp.where(
        iota(drop_ref.shape, 0) // (2 * order_k) == iota(drop_ref.shape, 1) // order_k, dropped, 0.0
    )


def tree_kernel(last, part_count, came_from, *refs):
    parts = refs[:part_count]
    mats_ref, lift_ref, drop_ref = refs[part_count : part_count + 3]
    rest = refs[part_count + 3 :]
    gathered = parts[0][...].astype(jnp.float32)
    for part in parts[1:]:
        gathered = gathered + part[...].astype(jnp.float32)
    boxes, order_k, plane = gathered.shape
    parent_count = boxes // 8

    def matrix(n):
        return mats_ref[n, 0], mats_ref[n, 1]

    summed = None
    for quad in range(4):
        stacked = jnp.concatenate(
            [gathered[8 * p + 4 * c + quad] for p in range(parent_count) for c in range(2)], axis=0
        )
        inner = mm_halves(halves(stacked), matrix(quad))
        summed = inner if summed is None else summed + inner
    own = mm_halves(halves(lift_ref[...]), halves(summed))
    dropped_x = halves(mm_halves(halves(drop_ref[...]), halves(own)))
    dropped = [mm_halves(dropped_x, matrix(4 + quad)) for quad in range(4)]
    fields = []
    for b in range(boxes):
        start = (b // 4) * order_k
        fields.append(gathered[b] - dropped[b % 4][start : start + order_k])
    if last:
        field_ref, parent_ref = rest
        if field_ref.shape[0] > boxes:
            field_ref[...] = jnp.zeros_like(field_ref)
        for b in range(boxes):
            field_ref[came_from[b]] = fields[b].astype(field_ref.dtype)
        for p in range(parent_count):
            for i in range(order_k):
                parent_ref[p : p + 1, i * plane : (i + 1) * plane] = own[p * order_k + i : p * order_k + i + 1]
    else:
        pot_ref, out_ref = rest
        potential = jnp.concatenate([pot_ref[came_from[b]] for b in range(boxes)], axis=0).astype(jnp.float32)
        current = halves(jnp.concatenate(fields, axis=0))
        values = mm_halves(matrix(10), halves(mm_halves(current, matrix(8))))
        product = values * (potential + 0.25 * values * values)
        source = mm_halves(matrix(11), halves(mm_halves(halves(product), matrix(9))))
        out_ref[...] = source.astype(jnp.bfloat16).reshape(out_ref.shape)


def unpack_kernel(parent_of, field_ref, out_ref):
    peers, order_k, plane = field_ref.shape
    boxes = out_ref.shape[0]
    for b in range(boxes):
        box = field_ref[parent_of[b] * 8 // boxes % peers].astype(jnp.float32)
        for x in range(order_k):
            out_ref[b : b + 1, x * plane : (x + 1) * plane] = box[x : x + 1]


def conv_kernel(dims, packed, *refs):
    term_count, order_k, disp_count, source_count, dest_count = dims
    source_refs = refs[:source_count]
    xl_ref, w_ref = refs[source_count : source_count + 2]
    out_refs = refs[source_count + 2 : source_count + 2 + dest_count]
    pbuf, total, held, held_sems = refs[source_count + 2 + dest_count :]
    plane = order_k * order_k
    list_rows = packed.shape[0] - 7
    half = term_count // 2
    depth = term_count * order_k
    block_boxes = out_refs[0].shape[0]
    dest_rows = dest_count * block_boxes
    loads = [
        pltpu.make_async_copy(ref, held.at[pl.ds(n * block_boxes, block_boxes)], held_sems.at[n])
        for n, ref in enumerate(source_refs)
    ]
    for load in loads:
        load.start()
    total[...] = jnp.zeros_like(total)
    for load in loads:
        load.wait()

    def push_w(ll, j, reg):
        for unit in range(2):
            column = pl.multiple_of(((unit * half + j) * disp_count + ll) * plane, plane)
            pltpu.matmul_push_rhs(w_ref[:, pl.ds(column, plane)], reg, unit)

    def block_body(ll, base, live, slots):
        pl.run_scoped(
            functools.partial(with_accs, ll, base, live, slots),
            *[
                [
                    [pltpu.ACC(unit)((order_k, plane), jnp.float32) for _ in range(slots)]
                    for _ in range(max(2, min(half, 2 * BLOCK // slots)))
                ]
                for unit in range(2)
            ],
        )

    def with_accs(ll, base, live, slots, *accs):
        codes = [packed[(base + t) // LANES, (base + t) % LANES] for t in range(slots)]
        ids = [code // (4 * dest_rows) for code in codes]
        shifts = [(code // dest_rows) % 4 for code in codes]

        stages = len(accs[0])

        def take(j, t):
            for unit in range(2):
                row = (unit * half + j) * order_k + t * depth
                tile = pltpu.matmul_pop(accs[unit][j % stages][t])
                pbuf[row : row + order_k, :] = tile.astype(jnp.bfloat16)

        push_w(ll, 0, 0)
        for j in range(half):
            if j + 1 < half:
                push_w(ll, j + 1, (j + 1) % 2)
            for t in range(slots):
                lhs = held[ids[t]]
                for unit in range(2):
                    pltpu.matmul_acc_lhs(accs[unit][j % stages][t], lhs, j % 2 if t == 0 else None)
                if j + 1 >= stages:
                    take(j + 1 - stages, t)
        for j in range(half - stages + 1, half):
            for t in range(slots):
                take(j, t)

        tiles = GROUP * depth // plane
        groups = slots // GROUP

        def place(g):
            for s in range(GROUP):
                t = g * GROUP + s
                tile = pltpu.matmul_pop(accs[g % 2][0][t])
                dest = jnp.where(t < live, codes[t] % dest_rows, dest_rows)
                total[dest] = total[dest] + tile

        for g in range(groups):
            unit = g % 2
            for q in range(tiles):
                reg = q % 2
                pltpu.matmul_push_rhs(pbuf[pl.ds(g * GROUP * depth + q * plane, plane), :], reg, unit)
                first = True
                for s in range(GROUP):
                    if s * depth < (q + 1) * plane and (s + 1) * depth > q * plane:
                        t = g * GROUP + s
                        pltpu.matmul_acc_lhs(
                            accs[unit][0][t], xl_ref[shifts[t], q + s], reg if first else None
                        )
                        first = False
            if g >= 3:
                place(g - 3)
        for g in range(max(groups - 3, 0), groups):
            place(g)

    def per_disp(ll, carry):
        start, stop = packed[list_rows, ll], packed[list_rows, ll + 1]

        def per_block(blk, inner):
            base = start + blk * BLOCK
            live = jnp.minimum(stop - base, BLOCK)
            lax.switch(
                (live + GROUP - 1) // GROUP - 1,
                [functools.partial(block_body, ll, base, live, GROUP * (c + 1)) for c in range(BLOCK // GROUP)],
            )
            return inner

        lax.fori_loop(0, (stop - start + BLOCK - 1) // BLOCK, per_block, 0)
        return carry

    lax.fori_loop(0, disp_count, per_disp, 0)
    for r, out_ref in enumerate(out_refs):
        out_ref[...] = total[pl.ds(r * block_boxes, block_boxes)].astype(jnp.bfloat16)


def shifted_factors(x_kernels):
    term_count, stacked, order_k = x_kernels.shape
    plane = order_k * order_k
    depth = term_count * order_k
    flat = x_kernels.reshape(term_count, 3, order_k, order_k).transpose(1, 2, 0, 3).reshape(3, order_k, depth)
    padded = jnp.pad(flat, ((0, 0), (0, 0), (plane, plane)))
    parts = {}
    for q in range(GROUP * depth // plane):
        for s in range(GROUP):
            if s * depth < (q + 1) * plane and (s + 1) * depth > q * plane:
                low = plane + q * plane - s * depth
                parts[q + s] = padded[:, :, low : low + plane]
    return jnp.stack([parts[p] for p in range(len(parts))], axis=1)


def convolve(sources, shifted, held_kernels, packed, dest_count, term_count, order_k):
    plane = order_k * order_k
    block_boxes = sources[0].shape[0]
    disp_count = held_kernels.shape[1] // (term_count * plane)
    dims = (term_count, order_k, disp_count, len(sources), dest_count)
    tile = jax.ShapeDtypeStruct((block_boxes, order_k, plane), jnp.bfloat16)
    return pl.pallas_call(
        functools.partial(conv_kernel, dims),
        out_shape=[tile] * dest_count,
        in_specs=[SMEM] + [ANY] * len(sources) + [VMEM, VMEM],
        out_specs=[VMEM] * dest_count,
        scratch_shapes=[
            pltpu.VMEM((BLOCK * term_count * order_k, plane), jnp.bfloat16),
            pltpu.VMEM((dest_count * block_boxes + 1, order_k, plane), jnp.float32),
            pltpu.VMEM((len(sources) * block_boxes, order_k, plane), jnp.bfloat16),
            pltpu.SemaphoreType.DMA((len(sources),)),
        ],
        compiler_params=pltpu.CompilerParams(vmem_limit_bytes=11 * MIB),
        name="convolve",
    )(packed, *sources, shifted, held_kernels)


def flips(count, step):
    return [(i, i ^ step) for i in range(count)]


def gather_sources(source, lo_count):
    near = [source] + [lax.ppermute(source, "lo", flips(lo_count, r)) for r in range(1, lo_count)]
    return near + [lax.ppermute(block, "oct", flips(2, 1)) for block in near]


def shards(
    coefficients,
    potential,
    to_values,
    x_kernels,
    yz_kernels,
    two_scale,
    disp_ids,
    dest_box,
    parent_of,
    child_octant,
):
    box_count, slot_count = disp_ids.shape
    order_k = to_values.shape[0]
    plane = order_k * order_k
    term_count = x_kernels.shape[0]
    disp_rows = yz_kernels.shape[1] // (term_count * plane)
    oct_count, hi_count, lo_count = (lax.axis_size(name) for name in ("oct", "hi", "lo"))
    oct_here, hi_here, lo_here = (lax.axis_index(name) for name in ("oct", "hi", "lo"))
    sub_count = hi_count * lo_count
    devices_all = oct_count * sub_count
    info = jnp.stack([oct_here, hi_here, lo_here]).astype(jnp.int32)
    tile = (box_count, order_k, plane)
    peer_tiles = jax.ShapeDtypeStruct((sub_count, order_k, plane), jnp.bfloat16)

    words = pl.pallas_call(
        pack_kernel,
        out_shape=jax.ShapeDtypeStruct((devices_all, box_count // 2, LANES), jnp.int32),
        in_specs=[SMEM] * 2 + [VMEM] * 2,
        out_specs=VMEM,
        name="pack_tables",
    )(parent_of, child_octant, disp_ids, dest_box)
    words, coefficients = lax.optimization_barrier((words, coefficients))
    words = lax.all_to_all(words, ("oct", "hi", "lo"), 0, 0, tiled=True)

    source, send_potential = pl.pallas_call(
        first_kernel,
        out_shape=[jax.ShapeDtypeStruct(tile, jnp.bfloat16), peer_tiles],
        in_specs=[SMEM] + [VMEM] * 3,
        out_specs=[VMEM] * 2,
        scratch_shapes=[pltpu.VMEM(peer_tiles.shape, jnp.float32)],
        name="first_source",
    )(parent_of, coefficients, potential, to_values)

    parents = box_count // 8 * order_k
    source, late_values = lax.optimization_barrier((source, to_values))
    fixed = pl.pallas_call(
        constants_kernel,
        out_shape=[
            pltpu.VMEM((12, 2, plane, plane), jnp.bfloat16),
            jax.ShapeDtypeStruct((parents, 2 * parents), jnp.float32),
            jax.ShapeDtypeStruct((2 * parents, parents), jnp.float32),
        ],
        in_specs=[VMEM] * 2,
        out_specs=[VMEM] * 3,
        compiler_params=pltpu.CompilerParams(vmem_limit_bytes=16 * MIB),
        name="make_constants",
    )(late_values, two_scale)
    fixed = [pltpu.with_memory_space_constraint(fixed[0], pltpu.VMEM)] + list(fixed[1:])

    list_rows = -(-(oct_count * lo_count * box_count * slot_count // LANES + 8) // 8) * 8
    *lists, moved, held_kernels = pl.pallas_call(
        functools.partial(route_kernel, (oct_count, hi_count, lo_count, box_count, slot_count, disp_rows)),
        out_shape=[jax.ShapeDtypeStruct((list_rows, LANES), jnp.int32)] * ITERS
        + [
            jax.ShapeDtypeStruct((8, LANES), jnp.int32),
            pltpu.VMEM(yz_kernels.shape, yz_kernels.dtype),
        ],
        in_specs=[SMEM, VMEM, ANY],
        out_specs=[VMEM] * (ITERS + 2),
        scratch_shapes=[pltpu.SemaphoreType.DMA],
        compiler_params=pltpu.CompilerParams(vmem_limit_bytes=11 * MIB),
        name="route_slots",
    )(info, words, yz_kernels)
    held_kernels = pltpu.with_memory_space_constraint(held_kernels, pltpu.VMEM)
    lists, send_potential = lax.optimization_barrier((lists, send_potential))
    moved_potential = lax.all_to_all(send_potential, ("hi", "lo"), 0, 0, tiled=True)
    came_from = moved[1, :box_count] // box_count % sub_count
    shifted = shifted_factors(x_kernels)

    for iteration in range(ITERS):
        last = iteration == ITERS - 1
        sources = gather_sources(source, lo_count)
        outs = convolve(sources, shifted, held_kernels, lists[iteration], hi_count, term_count, order_k)
        parts = [outs[0]] + [lax.ppermute(outs[r], "hi", flips(hi_count, r)) for r in range(1, hi_count)]
        kernel = functools.partial(tree_kernel, last, hi_count)
        if last:
            fields, parents = pl.pallas_call(
                kernel,
                out_shape=[
                    peer_tiles,
                    jax.ShapeDtypeStruct((box_count // 8, order_k * plane), jnp.float32),
                ],
                in_specs=[SMEM] + [VMEM] * (hi_count + 3),
                out_specs=[VMEM] * 2,
                name="last_tree",
            )(came_from, *parts, *fixed)
        else:
            source = pl.pallas_call(
                kernel,
                out_shape=jax.ShapeDtypeStruct(tile, jnp.bfloat16),
                in_specs=[SMEM] + [VMEM] * (hi_count + 4),
                out_specs=VMEM,
                name="tree_source",
            )(came_from, *parts, *fixed, moved_potential)
    returned = lax.all_to_all(fields, ("hi", "lo"), 0, 0, tiled=True)
    next_field = pl.pallas_call(
        unpack_kernel,
        out_shape=jax.ShapeDtypeStruct((box_count, order_k * plane), jnp.float32),
        in_specs=[SMEM, VMEM],
        out_specs=VMEM,
        name="unpack_fields",
    )(parent_of, returned)
    return next_field, parents


def solution(mesh):
    oct_count, sub_count = mesh.devices.shape
    lo_count = 4
    split = Mesh(mesh.devices.reshape(oct_count, sub_count // lo_count, lo_count), ("oct", "hi", "lo"))
    rows = ("oct", "hi", "lo")
    placed = (
        P(rows, None),
        P(rows, None),
        P(),
        P(),
        P(),
        P(),
        P(rows, None),
        P(rows, None),
        P(rows),
        P(rows),
    )
    return jax.shard_map(
        shards,
        mesh=split,
        in_specs=placed,
        out_specs=(P(rows, None), P(rows, None)),
        check_vma=False,
    )
```

```python
import functools

import jax
import jax.numpy as jnp
from jax import lax
from jax.experimental import pallas as pl
from jax.experimental.pallas import tpu as pltpu
from jax.sharding import Mesh
from jax.sharding import PartitionSpec as P

ITERS = 2
BLOCK = 32
AHEAD = 3
GROUP = 4
LANES = 128
MIB = 1024 * 1024
SMEM = pl.BlockSpec(memory_space=pltpu.SMEM)
VMEM = pl.BlockSpec(memory_space=pltpu.VMEM)
ANY = pl.BlockSpec(memory_space=pl.ANY)


def iota(shape, dim):
    return lax.broadcasted_iota(jnp.int32, shape, dim)


def mm(left, right):
    return jnp.dot(left, right, precision=lax.Precision.HIGHEST, preferred_element_type=jnp.float32)


def dot16(left, right):
    return jnp.dot(left, right, preferred_element_type=jnp.float32)


def halves(matrix):
    high = matrix.astype(jnp.bfloat16)
    return high, (matrix - high.astype(jnp.float32)).astype(jnp.bfloat16)


def mm_halves(left, right):
    rows = left[0].shape[0]
    both = dot16(jnp.concatenate(left, axis=0), right[0])
    return both[:rows] + both[rows:] + dot16(left[0], right[1])


def rows_high(matrix):
    order_k, width = matrix.shape
    return jnp.broadcast_to(matrix[:, None, :], (order_k, order_k, width)).reshape(order_k * order_k, width)


def rows_low(matrix):
    order_k, width = matrix.shape
    return jnp.broadcast_to(matrix[None, :, :], (order_k, order_k, width)).reshape(order_k * order_k, width)


def spread_columns(matrix, flip=False):
    order_k = matrix.shape[0]
    shape = (order_k, order_k * order_k)
    slot, lane = iota(shape, 0), iota(shape, 1)
    high = (lane // order_k == slot).astype(jnp.float32)
    low = (lane % order_k == slot).astype(jnp.float32)
    if flip:
        matrix = matrix.T
    return mm(matrix, high), mm(matrix, low)


def masks(order_k):
    shape = (order_k * order_k, order_k * order_k)
    row, lane = iota(shape, 0), iota(shape, 1)
    return row // order_k, row % order_k, lane // order_k, lane % order_k


def pack_kernel(parent_of, octant, disp_ref, dest_ref, out_ref):
    boxes, slots = disp_ref.shape
    half = boxes // 2
    dest = dest_ref[...]
    entry = jnp.where(dest >= 0, dest * 32 + disp_ref[...] + 1, 0).astype(jnp.float32)
    lane = iota((slots, LANES), 1)
    slot = iota((slots, LANES), 0)
    lane_out = iota((half, LANES), 1)
    row_out = iota((half, LANES), 0)
    words = jnp.zeros((half, LANES), jnp.float32)
    for h in range(2):
        start = h * (LANES // 2)
        words += mm(entry[h * half : (h + 1) * half], (lane == slot + start).astype(jnp.float32))
    words = words.astype(jnp.int32)
    for b in range(boxes):
        here = (row_out == b % half) & (lane_out == b // half * (LANES // 2) + slots)
        words = jnp.where(here, parent_of[b] * 8 + octant[b], words)
    for d in range(out_ref.shape[0]):
        out_ref[d] = words


def first_kernel(parent_of, coef_ref, pot_ref, to_ref, out_ref, pot_out, rows_ref):
    order_k = to_ref.shape[0]
    plane = order_k * order_k
    to_high, to_low = spread_columns(to_ref[...])
    back_high, back_low = spread_columns(to_ref[...], True)
    row_high, row_low, lane_high, lane_low = masks(order_k)
    value_pair = halves(rows_high(back_high) * rows_low(back_low))
    back_pair = halves(rows_high(to_high) * rows_low(to_low))
    value_x = halves(jnp.where(row_low == lane_low, rows_high(to_high), 0.0))
    source_x = halves(jnp.where(row_high == lane_low, rows_low(back_high), 0.0))

    def by_x(ref):
        return jnp.concatenate([ref[:, x * plane : (x + 1) * plane] for x in range(order_k)], axis=0)

    values = mm_halves(value_x, halves(mm_halves(halves(by_x(coef_ref)), value_pair)))
    product = values * (by_x(pot_ref) + 0.25 * values * values)
    source = mm_halves(source_x, halves(mm_halves(halves(product), back_pair)))
    out_ref[...] = source.astype(jnp.bfloat16).reshape(out_ref.shape)
    peers = rows_ref.shape[0]
    if peers > pot_ref.shape[0]:
        rows_ref[...] = jnp.zeros_like(rows_ref)
    for b in range(pot_ref.shape[0]):
        peer = parent_of[b] * 8 // pot_ref.shape[0] % peers
        for x in range(order_k):
            rows_ref[peer, x : x + 1, :] = pot_ref[b : b + 1, x * plane : (x + 1) * plane]
    pot_out[...] = rows_ref[...].astype(jnp.bfloat16)


def route_kernel(dims, info, words_ref, *refs):
    oct_count, hi_count, lo_count, boxes, slots, disp_rows = dims
    list_refs, moved_ref = refs[:ITERS], refs[ITERS]
    oct_here, hi_here, lo_here = info[0], info[1], info[2]
    width = LANES // 2
    words = words_ref[...].reshape(-1, LANES)
    table = jnp.concatenate([words[:, :width], words[:, width:]], axis=0)
    total = table.shape[0]

    def box_id(row):
        member = row % (total // 2)
        return member // (boxes // 2) * boxes + row // (total // 2) * (boxes // 2) + member % (boxes // 2)

    place_col, id_col = table[:, slots : slots + 1], box_id(iota((total, 1), 0))
    flat = table.astype(jnp.float32).T.astype(jnp.int32)
    flat = jnp.where(iota(flat.shape, 0) == slots + 1, box_id(iota(flat.shape, 1)), flat)
    low = (flat % 256).astype(jnp.float32).astype(jnp.bfloat16)
    high = (flat // 256).astype(jnp.float32).astype(jnp.bfloat16)

    def look(hit):
        chosen = hit.astype(jnp.float32).astype(jnp.bfloat16)
        return (dot16(low, chosen) + 256.0 * dot16(high, chosen)).astype(jnp.int32)

    lanes = oct_count * lo_count * boxes
    lane = iota((1, lanes), 1)
    member = lane // boxes
    device = ((member // lo_count) ^ oct_here) * (hi_count * lo_count) + hi_here * lo_count
    device = device + ((member % lo_count) ^ lo_here)
    target = device * boxes + lane % boxes
    dest_rows = hi_count * boxes
    source = iota((slots, lanes), 1)
    list_rows = list_refs[0].shape[0]
    upper = (iota((lanes, lanes), 0) < iota((lanes, lanes), 1)).astype(jnp.float32).astype(jnp.bfloat16)
    ones = jnp.ones((lanes, lanes), jnp.bfloat16)
    ranks = disp_rows * slots
    lower = (iota((ranks, ranks), 1) < iota((ranks, ranks), 0)).astype(jnp.float32).astype(jnp.bfloat16)
    for it in range(ITERS):
        found = look((id_col if it == 0 else place_col) == target)
        if it == 1:
            moved_ref[...] = found[slots : slots + 8]
        entry = found[:slots] - 1
        dest = jnp.where(entry >= 0, entry // 32, -1)
        disp = jnp.maximum(entry, 0) % 32
        place = jnp.concatenate(
            [look(id_col == dest[s : s + 1])[slots : slots + 1] for s in range(slots)], axis=0
        )
        owner = place // boxes
        keep = (entry >= 0) & (owner // (hi_count * lo_count) == oct_here) & (owner % lo_count == lo_here)
        away = ((owner // lo_count) % hi_count) ^ hi_here
        shift = jnp.zeros_like(disp)
        for c in range(1, 3):
            shift += (disp >= c * disp_rows).astype(jnp.int32)
        row = disp - shift * disp_rows
        member_of = [keep & (row == g) for g in range(disp_rows)]
        marks = jnp.concatenate(member_of, axis=0).astype(jnp.float32).astype(jnp.bfloat16)
        sums = dot16(marks, ones)
        starts = dot16(lower, sums.astype(jnp.bfloat16))
        ordinal = (starts + dot16(marks, upper)).astype(jnp.int32)
        position = jnp.full((slots, lanes), -1, jnp.int32)
        for g in range(disp_rows):
            position = jnp.where(member_of[g], ordinal[g * slots : (g + 1) * slots], position)
        code = (source * 4 + shift) * dest_rows + away * boxes + place % boxes
        pieces = [((code // 256**n) % 256).astype(jnp.float32) for n in range(3)]
        listed = jnp.zeros((3 * list_rows, LANES), jnp.float32)
        for s in range(slots):
            spot = position[s : s + 1]
            in_row = (spot // LANES == iota((list_rows, lanes), 0)) & (spot >= 0)
            left = jnp.concatenate([jnp.where(in_row, piece[s : s + 1], 0.0) for piece in pieces], axis=0)
            in_lane = (spot % LANES == iota((LANES, lanes), 0)).astype(jnp.float32).astype(jnp.bfloat16)
            listed += lax.dot_general(
                left.astype(jnp.bfloat16), in_lane, (((1,), (1,)), ((), ())), preferred_element_type=jnp.float32
            )
        packed = sum(
            listed[n * list_rows : (n + 1) * list_rows].astype(jnp.int32) * 256**n for n in range(3)
        )
        bound = (starts[ranks - 1 : ranks] + sums[ranks - 1 : ranks]).astype(jnp.int32)
        for g in range(disp_rows):
            bound = jnp.where(lane == g, starts[g * slots : g * slots + 1].astype(jnp.int32), bound)
        list_refs[it][...] = jnp.where(iota(packed.shape, 0) == list_rows - 7, bound, packed)


def constants_kernel(to_ref, two_ref, mats_ref, lift_ref, drop_ref):
    order_k = to_ref.shape[0]
    to_high, to_low = spread_columns(to_ref[...])
    back_high, back_low = spread_columns(to_ref[...], True)
    two = [spread_columns(two_ref[c]) for c in range(2)]
    flip = [spread_columns(two_ref[c], True) for c in range(2)]
    row_high, row_low, lane_high, lane_low = masks(order_k)
    made = []
    for quad in range(4):
        made.append(rows_high(flip[quad // 2][0]) * rows_low(flip[quad % 2][1]))
    for quad in range(4):
        made.append(rows_high(two[quad // 2][0]) * rows_low(two[quad % 2][1]))
    made.append(rows_high(back_high) * rows_low(back_low))
    made.append(rows_high(to_high) * rows_low(to_low))
    made.append(jnp.where(row_high == lane_high, rows_low(to_low), 0.0))
    made.append(jnp.where(row_high == lane_high, rows_low(back_low), 0.0))
    for n, matrix in enumerate(made):
        mats_ref[n, 0], mats_ref[n, 1] = halves(matrix)
    parents, wide = lift_ref.shape
    shape = (order_k, wide)
    lifted = jnp.zeros(shape, jnp.float32)
    for c in range(2):
        hot = (iota(shape, 1) % order_k == iota(shape, 0)) & ((iota(shape, 1) // order_k) % 2 == c)
        lifted += mm(two_ref[c], hot.astype(jnp.float32))
    lifted = jnp.concatenate([lifted] * (parents // order_k), axis=0)
    lift_ref[...] = jnp.where(
        iota(lift_ref.shape, 0) // order_k == iota(lift_ref.shape, 1) // (2 * order_k), lifted, 0.0
    )
    hot = (iota((order_k, parents), 1) % order_k == iota((order_k, parents), 0)).astype(jnp.float32)
    dropped = jnp.concatenate([mm(two_ref[c].T, hot) for c in range(2)] * (parents // order_k), axis=0)
    drop_ref[...] = jnp.where(
        iota(drop_ref.shape, 0) // (2 * order_k) == iota(drop_ref.shape, 1) // order_k, dropped, 0.0
    )


def tree_kernel(last, part_count, came_from, *refs):
    parts = refs[:part_count]
    mats_ref, lift_ref, drop_ref = refs[part_count : part_count + 3]
    rest = refs[part_count + 3 :]
    gathered = parts[0][...].astype(jnp.float32)
    for part in parts[1:]:
        gathered = gathered + part[...].astype(jnp.float32)
    boxes, order_k, plane = gathered.shape
    parent_count = boxes // 8

    def matrix(n):
        return mats_ref[n, 0], mats_ref[n, 1]

    summed = None
    for quad in range(4):
        stacked = jnp.concatenate(
            [gathered[8 * p + 4 * c + quad] for p in range(parent_count) for c in range(2)], axis=0
        )
        inner = mm_halves(halves(stacked), matrix(quad))
        summed = inner if summed is None else summed + inner
    own = mm_halves(halves(lift_ref[...]), halves(summed))
    dropped_x = halves(mm_halves(halves(drop_ref[...]), halves(own)))
    dropped = [mm_halves(dropped_x, matrix(4 + quad)) for quad in range(4)]
    fields = []
    for b in range(boxes):
        start = (b // 4) * order_k
        fields.append(gathered[b] - dropped[b % 4][start : start + order_k])
    if last:
        field_ref, parent_ref = rest
        if field_ref.shape[0] > boxes:
            field_ref[...] = jnp.zeros_like(field_ref)
        for b in range(boxes):
            field_ref[came_from[b]] = fields[b].astype(field_ref.dtype)
        for p in range(parent_count):
            for i in range(order_k):
                parent_ref[p : p + 1, i * plane : (i + 1) * plane] = own[p * order_k + i : p * order_k + i + 1]
    else:
        pot_ref, out_ref = rest
        potential = jnp.concatenate([pot_ref[came_from[b]] for b in range(boxes)], axis=0).astype(jnp.float32)
        current = halves(jnp.concatenate(fields, axis=0))
        values = mm_halves(matrix(10), halves(mm_halves(current, matrix(8))))
        product = values * (potential + 0.25 * values * values)
        source = mm_halves(matrix(11), halves(mm_halves(halves(product), matrix(9))))
        out_ref[...] = source.astype(jnp.bfloat16).reshape(out_ref.shape)


def unpack_kernel(parent_of, field_ref, out_ref):
    peers, order_k, plane = field_ref.shape
    boxes = out_ref.shape[0]
    for b in range(boxes):
        box = field_ref[parent_of[b] * 8 // boxes % peers].astype(jnp.float32)
        for x in range(order_k):
            out_ref[b : b + 1, x * plane : (x + 1) * plane] = box[x : x + 1]


def conv_kernel(dims, packed, *refs):
    term_count, order_k, disp_count, source_count, dest_count = dims
    source_refs = refs[:source_count]
    xl_ref, w_hbm = refs[source_count : source_count + 2]
    out_refs = refs[source_count + 2 : source_count + 2 + dest_count]
    wbuf, pbuf, total, held, sems, held_sems = refs[source_count + 2 + dest_count :]
    plane = order_k * order_k
    list_rows = packed.shape[0] - 7
    half = term_count // 2
    depth = term_count * order_k
    block_boxes = out_refs[0].shape[0]
    dest_rows = dest_count * block_boxes
    loads = [
        pltpu.make_async_copy(ref, held.at[pl.ds(n * block_boxes, block_boxes)], held_sems.at[n])
        for n, ref in enumerate(source_refs)
    ]
    for load in loads:
        load.start()

    def load_row(ll):
        for m in range(term_count):
            column = pl.multiple_of((m * disp_count + ll) * plane, plane)
            pltpu.make_async_copy(w_hbm.at[:, pl.ds(column, plane)], wbuf.at[ll, m], sems.at[ll]).start()

    for ll in range(AHEAD):
        load_row(ll)
    total[...] = jnp.zeros_like(total)
    for load in loads:
        load.wait()

    def push_w(ll, j, reg):
        for unit in range(2):
            pltpu.matmul_push_rhs(wbuf[ll, unit * half + j], reg, unit)

    def block_body(ll, base, live, slots):
        pl.run_scoped(
            functools.partial(with_accs, ll, base, live, slots),
            *[
                [
                    [pltpu.ACC(unit)((order_k, plane), jnp.float32) for _ in range(slots)]
                    for _ in range(max(2, min(half, 2 * BLOCK // slots)))
                ]
                for unit in range(2)
            ],
        )

    def with_accs(ll, base, live, slots, *accs):
        codes = [packed[(base + t) // LANES, (base + t) % LANES] for t in range(slots)]
        ids = [code // (4 * dest_rows) for code in codes]
        shifts = [(code // dest_rows) % 4 for code in codes]

        stages = len(accs[0])

        def take(j, t):
            for unit in range(2):
                row = (unit * half + j) * order_k + t * depth
                tile = pltpu.matmul_pop(accs[unit][j % stages][t])
                pbuf[row : row + order_k, :] = tile.astype(jnp.bfloat16)

        push_w(ll, 0, 0)
        for j in range(half):
            if j + 1 < half:
                push_w(ll, j + 1, (j + 1) % 2)
            for t in range(slots):
                lhs = held[ids[t]]
                for unit in range(2):
                    pltpu.matmul_acc_lhs(accs[unit][j % stages][t], lhs, j % 2 if t == 0 else None)
                if j + 1 >= stages:
                    take(j + 1 - stages, t)
        for j in range(half - stages + 1, half):
            for t in range(slots):
                take(j, t)

        tiles = GROUP * depth // plane
        groups = slots // GROUP

        def place(g):
            for s in range(GROUP):
                t = g * GROUP + s
                tile = pltpu.matmul_pop(accs[g % 2][0][t])
                dest = jnp.where(t < live, codes[t] % dest_rows, dest_rows)
                total[dest] = total[dest] + tile

        for g in range(groups):
            unit = g % 2
            for q in range(tiles):
                reg = q % 2
                pltpu.matmul_push_rhs(pbuf[pl.ds(g * GROUP * depth + q * plane, plane), :], reg, unit)
                first = True
                for s in range(GROUP):
                    if s * depth < (q + 1) * plane and (s + 1) * depth > q * plane:
                        t = g * GROUP + s
                        pltpu.matmul_acc_lhs(
                            accs[unit][0][t], xl_ref[shifts[t], q + s], reg if first else None
                        )
                        first = False
            if g >= 3:
                place(g - 3)
        for g in range(max(groups - 3, 0), groups):
            place(g)

    def per_disp(ll, carry):
        @pl.when(ll + AHEAD < disp_count)
        def _():
            load_row(ll + AHEAD)

        pltpu.make_async_copy(wbuf.at[ll], wbuf.at[ll], sems.at[ll]).wait()
        start, stop = packed[list_rows, ll], packed[list_rows, ll + 1]

        def per_block(blk, inner):
            base = start + blk * BLOCK
            live = jnp.minimum(stop - base, BLOCK)
            lax.switch(
                (live + GROUP - 1) // GROUP - 1,
                [functools.partial(block_body, ll, base, live, GROUP * (c + 1)) for c in range(BLOCK // GROUP)],
            )
            return inner

        lax.fori_loop(0, (stop - start + BLOCK - 1) // BLOCK, per_block, 0)
        return carry

    lax.fori_loop(0, disp_count, per_disp, 0)
    for r, out_ref in enumerate(out_refs):
        out_ref[...] = total[pl.ds(r * block_boxes, block_boxes)].astype(jnp.bfloat16)


def shifted_factors(x_kernels):
    term_count, stacked, order_k = x_kernels.shape
    plane = order_k * order_k
    depth = term_count * order_k
    flat = x_kernels.reshape(term_count, 3, order_k, order_k).transpose(1, 2, 0, 3).reshape(3, order_k, depth)
    padded = jnp.pad(flat, ((0, 0), (0, 0), (plane, plane)))
    parts = {}
    for q in range(GROUP * depth // plane):
        for s in range(GROUP):
            if s * depth < (q + 1) * plane and (s + 1) * depth > q * plane:
                low = plane + q * plane - s * depth
                parts[q + s] = padded[:, :, low : low + plane]
    return jnp.stack([parts[p] for p in range(len(parts))], axis=1)


def convolve(sources, shifted, yz_kernels, packed, dest_count, term_count, order_k):
    plane = order_k * order_k
    block_boxes = sources[0].shape[0]
    disp_count = yz_kernels.shape[1] // (term_count * plane)
    dims = (term_count, order_k, disp_count, len(sources), dest_count)
    tile = jax.ShapeDtypeStruct((block_boxes, order_k, plane), jnp.bfloat16)
    return pl.pallas_call(
        functools.partial(conv_kernel, dims),
        out_shape=[tile] * dest_count,
        in_specs=[SMEM] + [ANY] * len(sources) + [VMEM, ANY],
        out_specs=[VMEM] * dest_count,
        scratch_shapes=[
            pltpu.VMEM((disp_count, term_count, plane, plane), jnp.bfloat16),
            pltpu.VMEM((BLOCK * term_count * order_k, plane), jnp.bfloat16),
            pltpu.VMEM((dest_count * block_boxes + 1, order_k, plane), jnp.float32),
            pltpu.VMEM((len(sources) * block_boxes, order_k, plane), jnp.bfloat16),
            pltpu.SemaphoreType.DMA((disp_count,)),
            pltpu.SemaphoreType.DMA((len(sources),)),
        ],
        compiler_params=pltpu.CompilerParams(vmem_limit_bytes=40 * MIB),
        name="convolve",
    )(packed, *sources, shifted, yz_kernels)


def flips(count, step):
    return [(i, i ^ step) for i in range(count)]


def gather_sources(source, lo_count):
    near = [source] + [lax.ppermute(source, "lo", flips(lo_count, r)) for r in range(1, lo_count)]
    return near + [lax.ppermute(block, "oct", flips(2, 1)) for block in near]


def shards(
    coefficients,
    potential,
    to_values,
    x_kernels,
    yz_kernels,
    two_scale,
    disp_ids,
    dest_box,
    parent_of,
    child_octant,
):
    box_count, slot_count = disp_ids.shape
    order_k = to_values.shape[0]
    plane = order_k * order_k
    term_count = x_kernels.shape[0]
    disp_rows = yz_kernels.shape[1] // (term_count * plane)
    oct_count, hi_count, lo_count = (lax.axis_size(name) for name in ("oct", "hi", "lo"))
    oct_here, hi_here, lo_here = (lax.axis_index(name) for name in ("oct", "hi", "lo"))
    sub_count = hi_count * lo_count
    devices_all = oct_count * sub_count
    info = jnp.stack([oct_here, hi_here, lo_here]).astype(jnp.int32)
    tile = (box_count, order_k, plane)
    peer_tiles = jax.ShapeDtypeStruct((sub_count, order_k, plane), jnp.bfloat16)

    words = pl.pallas_call(
        pack_kernel,
        out_shape=jax.ShapeDtypeStruct((devices_all, box_count // 2, LANES), jnp.int32),
        in_specs=[SMEM] * 2 + [VMEM] * 2,
        out_specs=VMEM,
        name="pack_tables",
    )(parent_of, child_octant, disp_ids, dest_box)
    words, coefficients = lax.optimization_barrier((words, coefficients))
    words = lax.all_to_all(words, ("oct", "hi", "lo"), 0, 0, tiled=True)

    source, send_potential = pl.pallas_call(
        first_kernel,
        out_shape=[jax.ShapeDtypeStruct(tile, jnp.bfloat16), peer_tiles],
        in_specs=[SMEM] + [VMEM] * 3,
        out_specs=[VMEM] * 2,
        scratch_shapes=[pltpu.VMEM(peer_tiles.shape, jnp.float32)],
        name="first_source",
    )(parent_of, coefficients, potential, to_values)

    parents = box_count // 8 * order_k
    source, late_values = lax.optimization_barrier((source, to_values))
    fixed = pl.pallas_call(
        constants_kernel,
        out_shape=[
            pltpu.VMEM((12, 2, plane, plane), jnp.bfloat16),
            jax.ShapeDtypeStruct((parents, 2 * parents), jnp.float32),
            jax.ShapeDtypeStruct((2 * parents, parents), jnp.float32),
        ],
        in_specs=[VMEM] * 2,
        out_specs=[VMEM] * 3,
        compiler_params=pltpu.CompilerParams(vmem_limit_bytes=16 * MIB),
        name="make_constants",
    )(late_values, two_scale)
    fixed = [pltpu.with_memory_space_constraint(fixed[0], pltpu.VMEM)] + list(fixed[1:])

    list_rows = -(-(oct_count * lo_count * box_count * slot_count // LANES + 8) // 8) * 8
    *lists, moved = pl.pallas_call(
        functools.partial(route_kernel, (oct_count, hi_count, lo_count, box_count, slot_count, disp_rows)),
        out_shape=[jax.ShapeDtypeStruct((list_rows, LANES), jnp.int32)] * ITERS
        + [
            jax.ShapeDtypeStruct((8, LANES), jnp.int32),
        ],
        in_specs=[SMEM, VMEM],
        out_specs=[VMEM] * (ITERS + 1),
        compiler_params=pltpu.CompilerParams(vmem_limit_bytes=11 * MIB),
        name="route_slots",
    )(info, words)
    came_from = moved[1, :box_count] // box_count % sub_count
    shifted = shifted_factors(x_kernels)

    for iteration in range(ITERS):
        last = iteration == ITERS - 1
        sources = gather_sources(source, lo_count)
        outs = convolve(sources, shifted, yz_kernels, lists[iteration], hi_count, term_count, order_k)
        parts = [outs[0]] + [lax.ppermute(outs[r], "hi", flips(hi_count, r)) for r in range(1, hi_count)]
        kernel = functools.partial(tree_kernel, last, hi_count)
        if last:
            fields, parents = pl.pallas_call(
                kernel,
                out_shape=[
                    peer_tiles,
                    jax.ShapeDtypeStruct((box_count // 8, order_k * plane), jnp.float32),
                ],
                in_specs=[SMEM] + [VMEM] * (hi_count + 3),
                out_specs=[VMEM] * 2,
                name="last_tree",
            )(came_from, *parts, *fixed)
        else:
            near, send_potential = lax.optimization_barrier((parts[1], send_potential))
            parts[1] = near
            moved_potential = lax.all_to_all(send_potential, ("hi", "lo"), 0, 0, tiled=True)
            source = pl.pallas_call(
                kernel,
                out_shape=jax.ShapeDtypeStruct(tile, jnp.bfloat16),
                in_specs=[SMEM] + [VMEM] * (hi_count + 4),
                out_specs=VMEM,
                name="tree_source",
            )(came_from, *parts, *fixed, moved_potential)
    returned = lax.all_to_all(fields, ("hi", "lo"), 0, 0, tiled=True)
    next_field = pl.pallas_call(
        unpack_kernel,
        out_shape=jax.ShapeDtypeStruct((box_count, order_k * plane), jnp.float32),
        in_specs=[SMEM, VMEM],
        out_specs=VMEM,
        name="unpack_fields",
    )(parent_of, returned)
    return next_field, parents


def solution(mesh):
    oct_count, sub_count = mesh.devices.shape
    lo_count = 4
    split = Mesh(mesh.devices.reshape(oct_count, sub_count // lo_count, lo_count), ("oct", "hi", "lo"))
    rows = ("oct", "hi", "lo")
    placed = (
        P(rows, None),
        P(rows, None),
        P(),
        P(),
        P(),
        P(),
        P(rows, None),
        P(rows, None),
        P(rows),
        P(rows),
    )
    return jax.shard_map(
        shards,
        mesh=split,
        in_specs=placed,
        out_specs=(P(rows, None), P(rows, None)),
        check_vma=False,
    )
```

```python
import functools

import jax
import jax.numpy as jnp
from jax import lax
from jax.experimental import pallas as pl
from jax.experimental.pallas import tpu as pltpu
from jax.sharding import Mesh
from jax.sharding import PartitionSpec as P

ITERS = 2
BLOCK = 32
GROUP = 4
LANES = 128
MIB = 1024 * 1024
SMEM = pl.BlockSpec(memory_space=pltpu.SMEM)
VMEM = pl.BlockSpec(memory_space=pltpu.VMEM)
ANY = pl.BlockSpec(memory_space=pl.ANY)


def iota(shape, dim):
    return lax.broadcasted_iota(jnp.int32, shape, dim)


def mm(left, right):
    return jnp.dot(left, right, precision=lax.Precision.HIGHEST, preferred_element_type=jnp.float32)


def dot16(left, right):
    return jnp.dot(left, right, preferred_element_type=jnp.float32)


def halves(matrix):
    high = matrix.astype(jnp.bfloat16)
    return high, (matrix - high.astype(jnp.float32)).astype(jnp.bfloat16)


def mm_halves(left, right):
    rows = left[0].shape[0]
    both = dot16(jnp.concatenate(left, axis=0), right[0])
    return both[:rows] + both[rows:] + dot16(left[0], right[1])


def rows_high(matrix):
    order_k, width = matrix.shape
    return jnp.broadcast_to(matrix[:, None, :], (order_k, order_k, width)).reshape(order_k * order_k, width)


def rows_low(matrix):
    order_k, width = matrix.shape
    return jnp.broadcast_to(matrix[None, :, :], (order_k, order_k, width)).reshape(order_k * order_k, width)


def spread_columns(matrix, flip=False):
    order_k = matrix.shape[0]
    shape = (order_k, order_k * order_k)
    slot, lane = iota(shape, 0), iota(shape, 1)
    high = (lane // order_k == slot).astype(jnp.float32)
    low = (lane % order_k == slot).astype(jnp.float32)
    if flip:
        matrix = matrix.T
    return mm(matrix, high), mm(matrix, low)


def masks(order_k):
    shape = (order_k * order_k, order_k * order_k)
    row, lane = iota(shape, 0), iota(shape, 1)
    return row // order_k, row % order_k, lane // order_k, lane % order_k


def pack_kernel(parent_of, octant, disp_ref, dest_ref, out_ref):
    boxes, slots = disp_ref.shape
    half = boxes // 2
    dest = dest_ref[...]
    entry = jnp.where(dest >= 0, dest * 32 + disp_ref[...] + 1, 0).astype(jnp.float32)
    lane = iota((slots, LANES), 1)
    slot = iota((slots, LANES), 0)
    lane_out = iota((half, LANES), 1)
    row_out = iota((half, LANES), 0)
    words = jnp.zeros((half, LANES), jnp.float32)
    for h in range(2):
        start = h * (LANES // 2)
        words += mm(entry[h * half : (h + 1) * half], (lane == slot + start).astype(jnp.float32))
    words = words.astype(jnp.int32)
    for b in range(boxes):
        here = (row_out == b % half) & (lane_out == b // half * (LANES // 2) + slots)
        words = jnp.where(here, parent_of[b] * 8 + octant[b], words)
    for d in range(out_ref.shape[0]):
        out_ref[d] = words


def first_kernel(parent_of, coef_ref, pot_ref, to_ref, out_ref, pot_out, rows_ref):
    order_k = to_ref.shape[0]
    plane = order_k * order_k
    to_high, to_low = spread_columns(to_ref[...])
    back_high, back_low = spread_columns(to_ref[...], True)
    row_high, row_low, lane_high, lane_low = masks(order_k)
    value_pair = halves(rows_high(back_high) * rows_low(back_low))
    back_pair = halves(rows_high(to_high) * rows_low(to_low))
    value_x = halves(jnp.where(row_low == lane_low, rows_high(to_high), 0.0))
    source_x = halves(jnp.where(row_high == lane_low, rows_low(back_high), 0.0))

    def by_x(ref):
        return jnp.concatenate([ref[:, x * plane : (x + 1) * plane] for x in range(order_k)], axis=0)

    values = mm_halves(value_x, halves(mm_halves(halves(by_x(coef_ref)), value_pair)))
    product = values * (by_x(pot_ref) + 0.25 * values * values)
    source = mm_halves(source_x, halves(mm_halves(halves(product), back_pair)))
    out_ref[...] = source.astype(jnp.bfloat16).reshape(out_ref.shape)
    peers = rows_ref.shape[0]
    if peers > pot_ref.shape[0]:
        rows_ref[...] = jnp.zeros_like(rows_ref)
    for b in range(pot_ref.shape[0]):
        peer = parent_of[b] * 8 // pot_ref.shape[0] % peers
        for x in range(order_k):
            rows_ref[peer, x : x + 1, :] = pot_ref[b : b + 1, x * plane : (x + 1) * plane]
    pot_out[...] = rows_ref[...].astype(jnp.bfloat16)


def route_kernel(dims, first, info, words_ref, *refs):
    oct_count, hi_count, lo_count, boxes, slots, disp_rows = dims
    oct_here, hi_here, lo_here = info[0], info[1], info[2]
    width = LANES // 2
    words = words_ref[...].reshape(-1, LANES)
    table = jnp.concatenate([words[:, :width], words[:, width:]], axis=0)
    total = table.shape[0]

    def box_id(row):
        member = row % (total // 2)
        return member // (boxes // 2) * boxes + row // (total // 2) * (boxes // 2) + member % (boxes // 2)

    place_col, id_col = table[:, slots : slots + 1], box_id(iota((total, 1), 0))
    flat = table.astype(jnp.float32).T.astype(jnp.int32)
    flat = jnp.where(iota(flat.shape, 0) == slots + 1, box_id(iota(flat.shape, 1)), flat)
    low = (flat % 256).astype(jnp.float32).astype(jnp.bfloat16)
    high = (flat // 256).astype(jnp.float32).astype(jnp.bfloat16)

    def look(hit):
        chosen = hit.astype(jnp.float32).astype(jnp.bfloat16)
        return (dot16(low, chosen) + 256.0 * dot16(high, chosen)).astype(jnp.int32)

    lanes = oct_count * lo_count * boxes
    lane = iota((1, lanes), 1)
    member = lane // boxes
    device = ((member // lo_count) ^ oct_here) * (hi_count * lo_count) + hi_here * lo_count
    device = device + ((member % lo_count) ^ lo_here)
    target = device * boxes + lane % boxes
    dest_rows = hi_count * boxes
    source = iota((slots, lanes), 1)
    list_ref = refs[0] if first else refs[1]
    list_rows = list_ref.shape[0]
    upper = (iota((lanes, lanes), 0) < iota((lanes, lanes), 1)).astype(jnp.float32).astype(jnp.bfloat16)
    ones = jnp.ones((lanes, lanes), jnp.bfloat16)
    ranks = disp_rows * slots
    lower = (iota((ranks, ranks), 1) < iota((ranks, ranks), 0)).astype(jnp.float32).astype(jnp.bfloat16)
    if first:
        found = look(id_col == target)
        refs[1][...] = look(place_col == target)[: slots + 8]
    else:
        found = refs[0][...]
    entry = found[:slots] - 1
    dest = jnp.where(entry >= 0, entry // 32, -1)
    disp = jnp.maximum(entry, 0) % 32
    place = jnp.concatenate(
        [look(id_col == dest[s : s + 1])[slots : slots + 1] for s in range(slots)], axis=0
    )
    owner = place // boxes
    keep = (entry >= 0) & (owner // (hi_count * lo_count) == oct_here) & (owner % lo_count == lo_here)
    away = ((owner // lo_count) % hi_count) ^ hi_here
    shift = jnp.zeros_like(disp)
    for c in range(1, 3):
        shift += (disp >= c * disp_rows).astype(jnp.int32)
    row = disp - shift * disp_rows
    member_of = [keep & (row == g) for g in range(disp_rows)]
    marks = jnp.concatenate(member_of, axis=0).astype(jnp.float32).astype(jnp.bfloat16)
    sums = dot16(marks, ones)
    starts = dot16(lower, sums.astype(jnp.bfloat16))
    ordinal = (starts + dot16(marks, upper)).astype(jnp.int32)
    position = jnp.full((slots, lanes), -1, jnp.int32)
    for g in range(disp_rows):
        position = jnp.where(member_of[g], ordinal[g * slots : (g + 1) * slots], position)
    code = (source * 4 + shift) * dest_rows + away * boxes + place % boxes
    pieces = [((code // 256**n) % 256).astype(jnp.float32) for n in range(3)]
    listed = jnp.zeros((3 * list_rows, LANES), jnp.float32)
    for s in range(slots):
        spot = position[s : s + 1]
        in_row = (spot // LANES == iota((list_rows, lanes), 0)) & (spot >= 0)
        left = jnp.concatenate([jnp.where(in_row, piece[s : s + 1], 0.0) for piece in pieces], axis=0)
        in_lane = (spot % LANES == iota((LANES, lanes), 0)).astype(jnp.float32).astype(jnp.bfloat16)
        listed += lax.dot_general(
            left.astype(jnp.bfloat16), in_lane, (((1,), (1,)), ((), ())), preferred_element_type=jnp.float32
        )
    packed = sum(
        listed[n * list_rows : (n + 1) * list_rows].astype(jnp.int32) * 256**n for n in range(3)
    )
    bound = (starts[ranks - 1 : ranks] + sums[ranks - 1 : ranks]).astype(jnp.int32)
    for g in range(disp_rows):
        bound = jnp.where(lane == g, starts[g * slots : g * slots + 1].astype(jnp.int32), bound)
    list_ref[...] = jnp.where(iota(packed.shape, 0) == list_rows - 7, bound, packed)


def constants_kernel(to_ref, two_ref, mats_ref, lift_ref, drop_ref):
    order_k = to_ref.shape[0]
    to_high, to_low = spread_columns(to_ref[...])
    back_high, back_low = spread_columns(to_ref[...], True)
    two = [spread_columns(two_ref[c]) for c in range(2)]
    flip = [spread_columns(two_ref[c], True) for c in range(2)]
    row_high, row_low, lane_high, lane_low = masks(order_k)
    made = []
    for quad in range(4):
        made.append(rows_high(flip[quad // 2][0]) * rows_low(flip[quad % 2][1]))
    for quad in range(4):
        made.append(rows_high(two[quad // 2][0]) * rows_low(two[quad % 2][1]))
    made.append(rows_high(back_high) * rows_low(back_low))
    made.append(rows_high(to_high) * rows_low(to_low))
    made.append(jnp.where(row_high == lane_high, rows_low(to_low), 0.0))
    made.append(jnp.where(row_high == lane_high, rows_low(back_low), 0.0))
    for n, matrix in enumerate(made):
        mats_ref[n, 0], mats_ref[n, 1] = halves(matrix)
    parents, wide = lift_ref.shape
    shape = (order_k, wide)
    lifted = jnp.zeros(shape, jnp.float32)
    for c in range(2):
        hot = (iota(shape, 1) % order_k == iota(shape, 0)) & ((iota(shape, 1) // order_k) % 2 == c)
        lifted += mm(two_ref[c], hot.astype(jnp.float32))
    lifted = jnp.concatenate([lifted] * (parents // order_k), axis=0)
    lift_ref[...] = jnp.where(
        iota(lift_ref.shape, 0) // order_k == iota(lift_ref.shape, 1) // (2 * order_k), lifted, 0.0
    )
    hot = (iota((order_k, parents), 1) % order_k == iota((order_k, parents), 0)).astype(jnp.float32)
    dropped = jnp.concatenate([mm(two_ref[c].T, hot) for c in range(2)] * (parents // order_k), axis=0)
    drop_ref[...] = jnp.where(
        iota(drop_ref.shape, 0) // (2 * order_k) == iota(drop_ref.shape, 1) // order_k, dropped, 0.0
    )


def tree_kernel(last, part_count, came_from, *refs):
    parts = refs[:part_count]
    mats_ref, lift_ref, drop_ref = refs[part_count : part_count + 3]
    rest = refs[part_count + 3 :]
    gathered = parts[0][...].astype(jnp.float32)
    for part in parts[1:]:
        gathered = gathered + part[...].astype(jnp.float32)
    boxes, order_k, plane = gathered.shape
    parent_count = boxes // 8

    def matrix(n):
        return mats_ref[n, 0], mats_ref[n, 1]

    summed = None
    for quad in range(4):
        stacked = jnp.concatenate(
            [gathered[8 * p + 4 * c + quad] for p in range(parent_count) for c in range(2)], axis=0
        )
        inner = mm_halves(halves(stacked), matrix(quad))
        summed = inner if summed is None else summed + inner
    own = mm_halves(halves(lift_ref[...]), halves(summed))
    dropped_x = halves(mm_halves(halves(drop_ref[...]), halves(own)))
    dropped = [mm_halves(dropped_x, matrix(4 + quad)) for quad in range(4)]
    fields = []
    for b in range(boxes):
        start = (b // 4) * order_k
        fields.append(gathered[b] - dropped[b % 4][start : start + order_k])
    if last:
        field_ref, parent_ref = rest
        if field_ref.shape[0] > boxes:
            field_ref[...] = jnp.zeros_like(field_ref)
        for b in range(boxes):
            field_ref[came_from[b]] = fields[b].astype(field_ref.dtype)
        for p in range(parent_count):
            for i in range(order_k):
                parent_ref[p : p + 1, i * plane : (i + 1) * plane] = own[p * order_k + i : p * order_k + i + 1]
    else:
        pot_ref, out_ref = rest
        potential = jnp.concatenate([pot_ref[came_from[b]] for b in range(boxes)], axis=0).astype(jnp.float32)
        current = halves(jnp.concatenate(fields, axis=0))
        values = mm_halves(matrix(10), halves(mm_halves(current, matrix(8))))
        product = values * (potential + 0.25 * values * values)
        source = mm_halves(matrix(11), halves(mm_halves(halves(product), matrix(9))))
        out_ref[...] = source.astype(jnp.bfloat16).reshape(out_ref.shape)


def unpack_kernel(parent_of, field_ref, out_ref):
    peers, order_k, plane = field_ref.shape
    boxes = out_ref.shape[0]
    for b in range(boxes):
        box = field_ref[parent_of[b] * 8 // boxes % peers].astype(jnp.float32)
        for x in range(order_k):
            out_ref[b : b + 1, x * plane : (x + 1) * plane] = box[x : x + 1]


def conv_kernel(dims, packed, *refs):
    term_count, order_k, disp_count, source_count, dest_count = dims
    source_refs = refs[:source_count]
    xl_ref, w_hbm = refs[source_count : source_count + 2]
    out_refs = refs[source_count + 2 : source_count + 2 + dest_count]
    wbuf, pbuf, total, held, sems = refs[source_count + 2 + dest_count :]
    plane = order_k * order_k
    list_rows = packed.shape[0] - 7
    half = term_count // 2
    depth = term_count * order_k
    block_boxes = out_refs[0].shape[0]
    dest_rows = dest_count * block_boxes
    def load_row(ll):
        for m in range(term_count):
            column = pl.multiple_of((m * disp_count + ll) * plane, plane)
            pltpu.make_async_copy(w_hbm.at[:, pl.ds(column, plane)], wbuf.at[ll, m], sems.at[ll]).start()

    for ll in range(disp_count):
        load_row(ll)
    total[...] = jnp.zeros_like(total)
    for n, ref in enumerate(source_refs):
        held[pl.ds(n * block_boxes, block_boxes)] = ref[...]

    def push_w(ll, j, reg):
        for unit in range(2):
            pltpu.matmul_push_rhs(wbuf[ll, unit * half + j], reg, unit)

    def block_body(ll, base, live, slots):
        pl.run_scoped(
            functools.partial(with_accs, ll, base, live, slots),
            *[
                [
                    [pltpu.ACC(unit)((order_k, plane), jnp.float32) for _ in range(slots)]
                    for _ in range(max(2, min(half, 2 * BLOCK // slots)))
                ]
                for unit in range(2)
            ],
        )

    def with_accs(ll, base, live, slots, *accs):
        codes = [packed[(base + t) // LANES, (base + t) % LANES] for t in range(slots)]
        ids = [code // (4 * dest_rows) for code in codes]
        shifts = [(code // dest_rows) % 4 for code in codes]

        stages = len(accs[0])

        def take(j, t):
            for unit in range(2):
                row = (unit * half + j) * order_k + t * depth
                tile = pltpu.matmul_pop(accs[unit][j % stages][t])
                pbuf[row : row + order_k, :] = tile.astype(jnp.bfloat16)

        push_w(ll, 0, 0)
        for j in range(half):
            if j + 1 < half:
                push_w(ll, j + 1, (j + 1) % 2)
            for t in range(slots):
                lhs = held[ids[t]]
                for unit in range(2):
                    pltpu.matmul_acc_lhs(accs[unit][j % stages][t], lhs, j % 2 if t == 0 else None)
                if j + 1 >= stages:
                    take(j + 1 - stages, t)
        for j in range(half - stages + 1, half):
            for t in range(slots):
                take(j, t)

        tiles = GROUP * depth // plane
        groups = slots // GROUP

        def place(g):
            for s in range(GROUP):
                t = g * GROUP + s
                tile = pltpu.matmul_pop(accs[g % 2][0][t])
                dest = jnp.where(t < live, codes[t] % dest_rows, dest_rows)
                total[dest] = total[dest] + tile

        for g in range(groups):
            unit = g % 2
            for q in range(tiles):
                reg = q % 2
                pltpu.matmul_push_rhs(pbuf[pl.ds(g * GROUP * depth + q * plane, plane), :], reg, unit)
                first = True
                for s in range(GROUP):
                    if s * depth < (q + 1) * plane and (s + 1) * depth > q * plane:
                        t = g * GROUP + s
                        pltpu.matmul_acc_lhs(
                            accs[unit][0][t], xl_ref[shifts[t], q + s], reg if first else None
                        )
                        first = False
            if g >= 3:
                place(g - 3)
        for g in range(max(groups - 3, 0), groups):
            place(g)

    def per_disp(ll, carry):
        pltpu.make_async_copy(wbuf.at[ll], wbuf.at[ll], sems.at[ll]).wait()
        start, stop = packed[list_rows, ll], packed[list_rows, ll + 1]

        def per_block(blk, inner):
            base = start + blk * BLOCK
            live = jnp.minimum(stop - base, BLOCK)
            lax.switch(
                (live + GROUP - 1) // GROUP - 1,
                [functools.partial(block_body, ll, base, live, GROUP * (c + 1)) for c in range(BLOCK // GROUP)],
            )
            return inner

        lax.fori_loop(0, (stop - start + BLOCK - 1) // BLOCK, per_block, 0)
        return carry

    lax.fori_loop(0, disp_count, per_disp, 0)
    for r, out_ref in enumerate(out_refs):
        out_ref[...] = total[pl.ds(r * block_boxes, block_boxes)].astype(jnp.bfloat16)


def shifted_factors(x_kernels):
    term_count, stacked, order_k = x_kernels.shape
    plane = order_k * order_k
    depth = term_count * order_k
    flat = x_kernels.reshape(term_count, 3, order_k, order_k).transpose(1, 2, 0, 3).reshape(3, order_k, depth)
    padded = jnp.pad(flat, ((0, 0), (0, 0), (plane, plane)))
    parts = {}
    for q in range(GROUP * depth // plane):
        for s in range(GROUP):
            if s * depth < (q + 1) * plane and (s + 1) * depth > q * plane:
                low = plane + q * plane - s * depth
                parts[q + s] = padded[:, :, low : low + plane]
    return jnp.stack([parts[p] for p in range(len(parts))], axis=1)


def convolve(sources, shifted, yz_kernels, packed, dest_count, term_count, order_k):
    plane = order_k * order_k
    block_boxes = sources[0].shape[0]
    disp_count = yz_kernels.shape[1] // (term_count * plane)
    dims = (term_count, order_k, disp_count, len(sources), dest_count)
    tile = jax.ShapeDtypeStruct((block_boxes, order_k, plane), jnp.bfloat16)
    return pl.pallas_call(
        functools.partial(conv_kernel, dims),
        out_shape=[tile] * dest_count,
        in_specs=[SMEM] + [VMEM] * (len(sources) + 1) + [ANY],
        out_specs=[VMEM] * dest_count,
        scratch_shapes=[
            pltpu.VMEM((disp_count, term_count, plane, plane), jnp.bfloat16),
            pltpu.VMEM((BLOCK * term_count * order_k, plane), jnp.bfloat16),
            pltpu.VMEM((dest_count * block_boxes + 1, order_k, plane), jnp.float32),
            pltpu.VMEM((len(sources) * block_boxes, order_k, plane), jnp.bfloat16),
            pltpu.SemaphoreType.DMA((disp_count,)),
        ],
        compiler_params=pltpu.CompilerParams(vmem_limit_bytes=40 * MIB),
        name="convolve",
    )(packed, *sources, shifted, yz_kernels)


def flips(count, step):
    return [(i, i ^ step) for i in range(count)]


def gather_sources(source, lo_count):
    near = [source] + [lax.ppermute(source, "lo", flips(lo_count, r)) for r in range(1, lo_count)]
    return near + [lax.ppermute(block, "oct", flips(2, 1)) for block in near]


def shards(
    coefficients,
    potential,
    to_values,
    x_kernels,
    yz_kernels,
    two_scale,
    disp_ids,
    dest_box,
    parent_of,
    child_octant,
):
    box_count, slot_count = disp_ids.shape
    order_k = to_values.shape[0]
    plane = order_k * order_k
    term_count = x_kernels.shape[0]
    disp_rows = yz_kernels.shape[1] // (term_count * plane)
    oct_count, hi_count, lo_count = (lax.axis_size(name) for name in ("oct", "hi", "lo"))
    oct_here, hi_here, lo_here = (lax.axis_index(name) for name in ("oct", "hi", "lo"))
    sub_count = hi_count * lo_count
    devices_all = oct_count * sub_count
    info = jnp.stack([oct_here, hi_here, lo_here]).astype(jnp.int32)
    tile = (box_count, order_k, plane)
    peer_tiles = jax.ShapeDtypeStruct((sub_count, order_k, plane), jnp.bfloat16)

    words = pl.pallas_call(
        pack_kernel,
        out_shape=jax.ShapeDtypeStruct((devices_all, box_count // 2, LANES), jnp.int32),
        in_specs=[SMEM] * 2 + [VMEM] * 2,
        out_specs=VMEM,
        name="pack_tables",
    )(parent_of, child_octant, disp_ids, dest_box)
    words, coefficients = lax.optimization_barrier((words, coefficients))
    words = lax.all_to_all(words, ("oct", "hi", "lo"), 0, 0, tiled=True)

    source, send_potential = pl.pallas_call(
        first_kernel,
        out_shape=[jax.ShapeDtypeStruct(tile, jnp.bfloat16), peer_tiles],
        in_specs=[SMEM] + [VMEM] * 3,
        out_specs=[VMEM] * 2,
        scratch_shapes=[pltpu.VMEM(peer_tiles.shape, jnp.float32)],
        name="first_source",
    )(parent_of, coefficients, potential, to_values)

    parents = box_count // 8 * order_k
    source, late_values = lax.optimization_barrier((source, to_values))
    fixed = pl.pallas_call(
        constants_kernel,
        out_shape=[
            pltpu.VMEM((12, 2, plane, plane), jnp.bfloat16),
            jax.ShapeDtypeStruct((parents, 2 * parents), jnp.float32),
            jax.ShapeDtypeStruct((2 * parents, parents), jnp.float32),
        ],
        in_specs=[VMEM] * 2,
        out_specs=[VMEM] * 3,
        compiler_params=pltpu.CompilerParams(vmem_limit_bytes=16 * MIB),
        name="make_constants",
    )(late_values, two_scale)
    fixed = [pltpu.with_memory_space_constraint(fixed[0], pltpu.VMEM)] + list(fixed[1:])

    list_rows = -(-(oct_count * lo_count * box_count * slot_count // LANES + 8) // 8) * 8
    words, fixed = lax.optimization_barrier((words, fixed))
    sort_dims = (oct_count, hi_count, lo_count, box_count, slot_count, disp_rows)
    list_shape = jax.ShapeDtypeStruct((list_rows, LANES), jnp.int32)
    packed, found = pl.pallas_call(
        functools.partial(route_kernel, sort_dims, True),
        out_shape=[list_shape, jax.ShapeDtypeStruct((slot_count + 8, LANES), jnp.int32)],
        in_specs=[SMEM, VMEM],
        out_specs=[VMEM] * 2,
        compiler_params=pltpu.CompilerParams(vmem_limit_bytes=16 * MIB),
        name="route_slots",
    )(info, words)
    came_from = found[slot_count + 1, :box_count] // box_count % sub_count
    shifted = shifted_factors(x_kernels)

    for iteration in range(ITERS):
        last = iteration == ITERS - 1
        sources = gather_sources(source, lo_count)
        outs = convolve(sources, shifted, yz_kernels, packed, hi_count, term_count, order_k)
        if not last:
            outs, send_potential = lax.optimization_barrier((outs, send_potential))
        parts = [outs[0]] + [lax.ppermute(outs[r], "hi", flips(hi_count, r)) for r in range(1, hi_count)]
        kernel = functools.partial(tree_kernel, last, hi_count)
        if last:
            fields, parents = pl.pallas_call(
                kernel,
                out_shape=[
                    peer_tiles,
                    jax.ShapeDtypeStruct((box_count // 8, order_k * plane), jnp.float32),
                ],
                in_specs=[SMEM] + [VMEM] * (hi_count + 3),
                out_specs=[VMEM] * 2,
                name="last_tree",
            )(came_from, *parts, *fixed)
        else:
            moved_potential = lax.all_to_all(send_potential, ("hi", "lo"), 0, 0, tiled=True)
            source = pl.pallas_call(
                kernel,
                out_shape=jax.ShapeDtypeStruct(tile, jnp.bfloat16),
                in_specs=[SMEM] + [VMEM] * (hi_count + 4),
                out_specs=VMEM,
                name="tree_source",
            )(came_from, *parts, *fixed, moved_potential)
            source, words = lax.optimization_barrier((source, words))
            packed = pl.pallas_call(
                functools.partial(route_kernel, sort_dims, False),
                out_shape=list_shape,
                in_specs=[SMEM, VMEM, VMEM],
                out_specs=VMEM,
                compiler_params=pltpu.CompilerParams(vmem_limit_bytes=16 * MIB),
                name="route_again",
            )(info, words, found)
    returned = lax.all_to_all(fields, ("hi", "lo"), 0, 0, tiled=True)
    next_field = pl.pallas_call(
        unpack_kernel,
        out_shape=jax.ShapeDtypeStruct((box_count, order_k * plane), jnp.float32),
        in_specs=[SMEM, VMEM],
        out_specs=VMEM,
        name="unpack_fields",
    )(parent_of, returned)
    return next_field, parents


def solution(mesh):
    oct_count, sub_count = mesh.devices.shape
    lo_count = 4
    split = Mesh(mesh.devices.reshape(oct_count, sub_count // lo_count, lo_count), ("oct", "hi", "lo"))
    rows = ("oct", "hi", "lo")
    placed = (
        P(rows, None),
        P(rows, None),
        P(),
        P(),
        P(),
        P(),
        P(rows, None),
        P(rows, None),
        P(rows),
        P(rows),
    )
    return jax.shard_map(
        shards,
        mesh=split,
        in_specs=placed,
        out_specs=(P(rows, None), P(rows, None)),
        check_vma=False,
    )
```

```python
import functools

import jax
import jax.numpy as jnp
from jax import lax
from jax.experimental import pallas as pl
from jax.experimental.pallas import tpu as pltpu
from jax.sharding import Mesh
from jax.sharding import PartitionSpec as P

ITERS = 2
BLOCK = 32
TOTALS = 1
GROUP = 4
LANES = 128
MIB = 1024 * 1024
SMEM = pl.BlockSpec(memory_space=pltpu.SMEM)
VMEM = pl.BlockSpec(memory_space=pltpu.VMEM)
ANY = pl.BlockSpec(memory_space=pl.ANY)


def iota(shape, dim):
    return lax.broadcasted_iota(jnp.int32, shape, dim)


def mm(left, right):
    return jnp.dot(left, right, precision=lax.Precision.HIGHEST, preferred_element_type=jnp.float32)


def dot16(left, right):
    return jnp.dot(left, right, preferred_element_type=jnp.float32)


def halves(matrix):
    high = matrix.astype(jnp.bfloat16)
    return high, (matrix - high.astype(jnp.float32)).astype(jnp.bfloat16)


def mm_halves(left, right):
    rows = left[0].shape[0]
    both = dot16(jnp.concatenate(left, axis=0), right[0])
    return both[:rows] + both[rows:] + dot16(left[0], right[1])


def rows_high(matrix):
    order_k, width = matrix.shape
    return jnp.broadcast_to(matrix[:, None, :], (order_k, order_k, width)).reshape(order_k * order_k, width)


def rows_low(matrix):
    order_k, width = matrix.shape
    return jnp.broadcast_to(matrix[None, :, :], (order_k, order_k, width)).reshape(order_k * order_k, width)


def spread_columns(matrix):
    order_k = matrix.shape[0]
    plane = order_k * order_k
    slot, lane = iota((order_k, 2 * plane), 0), iota((order_k, 2 * plane), 1)
    chosen = jnp.where(lane < plane, lane // order_k, lane % order_k) == slot
    rows = jnp.concatenate(halves(matrix) + halves(matrix.T), axis=0)
    wide = dot16(rows, chosen.astype(jnp.float32).astype(jnp.bfloat16))
    plain = wide[:order_k] + wide[order_k : 2 * order_k]
    turned = wide[2 * order_k : 3 * order_k] + wide[3 * order_k :]
    return plain[:, :plane], plain[:, plane:], turned[:, :plane], turned[:, plane:]


def masks(order_k):
    shape = (order_k * order_k, order_k * order_k)
    row, lane = iota(shape, 0), iota(shape, 1)
    return row // order_k, row % order_k, lane // order_k, lane % order_k


def pack_kernel(parent_of, octant, disp_ref, dest_ref, out_ref):
    boxes, slots = disp_ref.shape
    half = boxes // 2
    dest = dest_ref[...]
    entry = jnp.where(dest >= 0, dest * 32 + disp_ref[...] + 1, 0).astype(jnp.float32)
    lane = iota((slots, LANES), 1)
    slot = iota((slots, LANES), 0)
    lane_out = iota((half, LANES), 1)
    row_out = iota((half, LANES), 0)
    words = jnp.zeros((half, LANES), jnp.float32)
    for h in range(2):
        start = h * (LANES // 2)
        words += mm(entry[h * half : (h + 1) * half], (lane == slot + start).astype(jnp.float32))
    words = words.astype(jnp.int32)
    for b in range(boxes):
        here = (row_out == b % half) & (lane_out == b // half * (LANES // 2) + slots)
        words = jnp.where(here, parent_of[b] * 8 + octant[b], words)
    for d in range(out_ref.shape[0]):
        out_ref[d] = words


def first_kernel(parent_of, coef_ref, pot_ref, to_ref, out_ref, pot_out, rows_ref):
    order_k = to_ref.shape[0]
    plane = order_k * order_k
    to_high, to_low, back_high, back_low = spread_columns(to_ref[...])
    row_high, row_low, lane_high, lane_low = masks(order_k)
    value_pair = halves(rows_high(back_high) * rows_low(back_low))
    back_pair = halves(rows_high(to_high) * rows_low(to_low))
    value_x = halves(jnp.where(row_low == lane_low, rows_high(to_high), 0.0))
    source_x = halves(jnp.where(row_high == lane_low, rows_low(back_high), 0.0))

    def by_x(ref):
        return jnp.concatenate([ref[:, x * plane : (x + 1) * plane] for x in range(order_k)], axis=0)

    values = mm_halves(value_x, halves(mm_halves(halves(by_x(coef_ref)), value_pair)))
    product = values * (by_x(pot_ref) + 0.25 * values * values)
    source = mm_halves(source_x, halves(mm_halves(halves(product), back_pair)))
    out_ref[...] = source.astype(jnp.bfloat16).reshape(out_ref.shape)
    peers = rows_ref.shape[0]
    if peers > pot_ref.shape[0]:
        rows_ref[...] = jnp.zeros_like(rows_ref)
    for b in range(pot_ref.shape[0]):
        peer = parent_of[b] * 8 // pot_ref.shape[0] % peers
        for x in range(order_k):
            rows_ref[peer, x : x + 1, :] = pot_ref[b : b + 1, x * plane : (x + 1) * plane]
    pot_out[...] = rows_ref[...].astype(jnp.bfloat16)


def route_kernel(dims, first, info, words_ref, *refs):
    oct_count, hi_count, lo_count, boxes, slots, disp_rows = dims
    oct_here, hi_here, lo_here = info[0], info[1], info[2]
    width = LANES // 2
    words = words_ref[...].reshape(-1, LANES)
    table = jnp.concatenate([words[:, :width], words[:, width:]], axis=0)
    total = table.shape[0]

    def box_id(row):
        member = row % (total // 2)
        return member // (boxes // 2) * boxes + row // (total // 2) * (boxes // 2) + member % (boxes // 2)

    place_col, id_col = table[:, slots : slots + 1], box_id(iota((total, 1), 0))
    flat = table.astype(jnp.float32).T.astype(jnp.int32)
    flat = jnp.where(iota(flat.shape, 0) == slots + 1, box_id(iota(flat.shape, 1)), flat)
    low = (flat % 256).astype(jnp.float32).astype(jnp.bfloat16)
    high = (flat // 256).astype(jnp.float32).astype(jnp.bfloat16)

    def look(hit):
        chosen = hit.astype(jnp.float32).astype(jnp.bfloat16)
        return (dot16(low, chosen) + 256.0 * dot16(high, chosen)).astype(jnp.int32)

    lanes = oct_count * lo_count * boxes
    lane = iota((1, lanes), 1)
    member = lane // boxes
    device = ((member // lo_count) ^ oct_here) * (hi_count * lo_count) + hi_here * lo_count
    device = device + ((member % lo_count) ^ lo_here)
    target = device * boxes + lane % boxes
    dest_rows = hi_count * boxes
    source = iota((slots, lanes), 1)
    list_ref = refs[0] if first else refs[1]
    list_rows = list_ref.shape[0]
    upper = (iota((lanes, lanes), 0) < iota((lanes, lanes), 1)).astype(jnp.float32).astype(jnp.bfloat16)
    ones = jnp.ones((lanes, lanes), jnp.bfloat16)
    ranks = disp_rows * slots
    lower = (iota((ranks, ranks), 1) < iota((ranks, ranks), 0)).astype(jnp.float32).astype(jnp.bfloat16)
    if first:
        found = look(id_col == target)
        refs[1][...] = look(place_col == target)[: slots + 8]
    else:
        found = refs[0][...]
    entry = found[:slots] - 1
    dest = jnp.where(entry >= 0, entry // 32, -1)
    disp = jnp.maximum(entry, 0) % 32
    place = jnp.concatenate(
        [look(id_col == dest[s : s + 1])[slots : slots + 1] for s in range(slots)], axis=0
    )
    owner = place // boxes
    keep = (entry >= 0) & (owner // (hi_count * lo_count) == oct_here) & (owner % lo_count == lo_here)
    away = ((owner // lo_count) % hi_count) ^ hi_here
    shift = jnp.zeros_like(disp)
    for c in range(1, 3):
        shift += (disp >= c * disp_rows).astype(jnp.int32)
    row = disp - shift * disp_rows
    member_of = [keep & (row == g) for g in range(disp_rows)]
    marks = jnp.concatenate(member_of, axis=0).astype(jnp.float32).astype(jnp.bfloat16)
    sums = dot16(marks, ones)
    starts = dot16(lower, sums.astype(jnp.bfloat16))
    ordinal = (starts + dot16(marks, upper)).astype(jnp.int32)
    position = jnp.full((slots, lanes), -1, jnp.int32)
    for g in range(disp_rows):
        position = jnp.where(member_of[g], ordinal[g * slots : (g + 1) * slots], position)
    code = (source * 4 + shift) * dest_rows + away * boxes + place % boxes
    pieces = [((code // 256**n) % 256).astype(jnp.float32) for n in range(3)]
    listed = jnp.zeros((3 * list_rows, LANES), jnp.float32)
    for s in range(slots):
        spot = position[s : s + 1]
        in_row = (spot // LANES == iota((list_rows, lanes), 0)) & (spot >= 0)
        left = jnp.concatenate([jnp.where(in_row, piece[s : s + 1], 0.0) for piece in pieces], axis=0)
        in_lane = (spot % LANES == iota((LANES, lanes), 0)).astype(jnp.float32).astype(jnp.bfloat16)
        listed += lax.dot_general(
            left.astype(jnp.bfloat16), in_lane, (((1,), (1,)), ((), ())), preferred_element_type=jnp.float32
        )
    packed = sum(
        listed[n * list_rows : (n + 1) * list_rows].astype(jnp.int32) * 256**n for n in range(3)
    )
    bound = (starts[ranks - 1 : ranks] + sums[ranks - 1 : ranks]).astype(jnp.int32)
    for g in range(disp_rows):
        bound = jnp.where(lane == g, starts[g * slots : g * slots + 1].astype(jnp.int32), bound)
    list_ref[...] = jnp.where(iota(packed.shape, 0) == list_rows - 7, bound, packed)


def constants_kernel(to_ref, two_ref, mats_ref, lift_ref, drop_ref):
    order_k = to_ref.shape[0]
    to_high, to_low, back_high, back_low = spread_columns(to_ref[...])
    spread = [spread_columns(two_ref[c]) for c in range(2)]
    two, flip = [four[:2] for four in spread], [four[2:] for four in spread]
    row_high, row_low, lane_high, lane_low = masks(order_k)
    made = []
    for quad in range(4):
        made.append(rows_high(flip[quad // 2][0]) * rows_low(flip[quad % 2][1]))
    for quad in range(4):
        made.append(rows_high(two[quad // 2][0]) * rows_low(two[quad % 2][1]))
    made.append(rows_high(back_high) * rows_low(back_low))
    made.append(rows_high(to_high) * rows_low(to_low))
    made.append(jnp.where(row_high == lane_high, rows_low(to_low), 0.0))
    made.append(jnp.where(row_high == lane_high, rows_low(back_low), 0.0))
    for n, matrix in enumerate(made):
        mats_ref[n, 0], mats_ref[n, 1] = halves(matrix)
    parents, wide = lift_ref.shape
    shape = (order_k, wide)
    lifted = jnp.zeros(shape, jnp.float32)
    for c in range(2):
        hot = (iota(shape, 1) % order_k == iota(shape, 0)) & ((iota(shape, 1) // order_k) % 2 == c)
        lifted += mm(two_ref[c], hot.astype(jnp.float32))
    lifted = jnp.concatenate([lifted] * (parents // order_k), axis=0)
    lift_ref[...] = jnp.where(
        iota(lift_ref.shape, 0) // order_k == iota(lift_ref.shape, 1) // (2 * order_k), lifted, 0.0
    )
    hot = (iota((order_k, parents), 1) % order_k == iota((order_k, parents), 0)).astype(jnp.float32)
    dropped = jnp.concatenate([mm(two_ref[c].T, hot) for c in range(2)] * (parents // order_k), axis=0)
    drop_ref[...] = jnp.where(
        iota(drop_ref.shape, 0) // (2 * order_k) == iota(drop_ref.shape, 1) // order_k, dropped, 0.0
    )


def tree_kernel(last, part_count, came_from, *refs):
    parts = refs[:part_count]
    mats_ref, lift_ref, drop_ref = refs[part_count : part_count + 3]
    rest = refs[part_count + 3 :]
    gathered = parts[0][...].astype(jnp.float32)
    for part in parts[1:]:
        gathered = gathered + part[...].astype(jnp.float32)
    boxes, order_k, plane = gathered.shape
    parent_count = boxes // 8

    def matrix(n):
        return mats_ref[n, 0], mats_ref[n, 1]

    summed = None
    for quad in range(4):
        stacked = jnp.concatenate(
            [gathered[8 * p + 4 * c + quad] for p in range(parent_count) for c in range(2)], axis=0
        )
        inner = mm_halves(halves(stacked), matrix(quad))
        summed = inner if summed is None else summed + inner
    own = mm_halves(halves(lift_ref[...]), halves(summed))
    dropped_x = halves(mm_halves(halves(drop_ref[...]), halves(own)))
    dropped = [mm_halves(dropped_x, matrix(4 + quad)) for quad in range(4)]
    fields = []
    for b in range(boxes):
        start = (b // 4) * order_k
        fields.append(gathered[b] - dropped[b % 4][start : start + order_k])
    if last:
        field_ref, parent_ref = rest
        if field_ref.shape[0] > boxes:
            field_ref[...] = jnp.zeros_like(field_ref)
        for b in range(boxes):
            field_ref[came_from[b]] = fields[b].astype(field_ref.dtype)
        for p in range(parent_count):
            for i in range(order_k):
                parent_ref[p : p + 1, i * plane : (i + 1) * plane] = own[p * order_k + i : p * order_k + i + 1]
    else:
        pot_ref, out_ref = rest
        potential = jnp.concatenate([pot_ref[came_from[b]] for b in range(boxes)], axis=0).astype(jnp.float32)
        current = halves(jnp.concatenate(fields, axis=0))
        values = mm_halves(matrix(10), halves(mm_halves(current, matrix(8))))
        product = values * (potential + 0.25 * values * values)
        source = mm_halves(matrix(11), halves(mm_halves(halves(product), matrix(9))))
        out_ref[...] = source.astype(jnp.bfloat16).reshape(out_ref.shape)


def unpack_kernel(parent_of, field_ref, out_ref):
    peers, order_k, plane = field_ref.shape
    boxes = out_ref.shape[0]
    for b in range(boxes):
        box = field_ref[parent_of[b] * 8 // boxes % peers].astype(jnp.float32)
        for x in range(order_k):
            out_ref[b : b + 1, x * plane : (x + 1) * plane] = box[x : x + 1]


def conv_kernel(dims, packed, *refs):
    term_count, order_k, disp_count, source_count, dest_count = dims
    source_refs = refs[:source_count]
    xl_ref, w_hbm = refs[source_count : source_count + 2]
    out_refs = refs[source_count + 2 : source_count + 2 + dest_count]
    wbuf, pbuf, *totals, held, sems = refs[source_count + 2 + dest_count :]
    plane = order_k * order_k
    list_rows = packed.shape[0] - 7
    half = term_count // 2
    depth = term_count * order_k
    block_boxes = out_refs[0].shape[0]
    dest_rows = dest_count * block_boxes
    def load_row(ll):
        for m in range(term_count):
            column = pl.multiple_of((m * disp_count + ll) * plane, plane)
            pltpu.make_async_copy(w_hbm.at[:, pl.ds(column, plane)], wbuf.at[ll, m], sems.at[ll]).start()

    for ll in range(disp_count):
        load_row(ll)
    for total in totals:
        total[...] = jnp.zeros_like(total)
    for n, ref in enumerate(source_refs):
        held[pl.ds(n * block_boxes, block_boxes)] = ref[...]

    def push_w(ll, j, reg):
        for unit in range(2):
            pltpu.matmul_push_rhs(wbuf[ll, unit * half + j], reg, unit)

    def block_body(ll, base, live, slots):
        pl.run_scoped(
            functools.partial(with_accs, ll, base, live, slots),
            *[
                [
                    [pltpu.ACC(unit)((order_k, plane), jnp.float32) for _ in range(slots)]
                    for _ in range(max(2, min(half, 2 * BLOCK // slots)))
                ]
                for unit in range(2)
            ],
        )

    def with_accs(ll, base, live, slots, *accs):
        codes = [packed[(base + t) // LANES, (base + t) % LANES] for t in range(slots)]
        ids = [code // (4 * dest_rows) for code in codes]
        shifts = [(code // dest_rows) % 4 for code in codes]

        stages = len(accs[0])

        def take(j, t):
            for unit in range(2):
                row = (unit * half + j) * order_k + t * depth
                tile = pltpu.matmul_pop(accs[unit][j % stages][t])
                pbuf[row : row + order_k, :] = tile.astype(jnp.bfloat16)

        push_w(ll, 0, 0)
        for j in range(half):
            if j + 1 < half:
                push_w(ll, j + 1, (j + 1) % 2)
            for t in range(slots):
                lhs = held[ids[t]]
                for unit in range(2):
                    pltpu.matmul_acc_lhs(accs[unit][j % stages][t], lhs, j % 2 if t == 0 else None)
                if j + 1 >= stages:
                    take(j + 1 - stages, t)
        for j in range(half - stages + 1, half):
            for t in range(slots):
                take(j, t)

        tiles = GROUP * depth // plane
        groups = slots // GROUP

        def place(g):
            for s in range(GROUP):
                t = g * GROUP + s
                tile = pltpu.matmul_pop(accs[g % 2][0][t])
                total = totals[t % TOTALS]
                dest = jnp.where(t < live, codes[t] % dest_rows, dest_rows)
                total[dest] = total[dest] + tile

        for g in range(groups):
            unit = g % 2
            for q in range(tiles):
                reg = q % 2
                pltpu.matmul_push_rhs(pbuf[pl.ds(g * GROUP * depth + q * plane, plane), :], reg, unit)
                first = True
                for s in range(GROUP):
                    if s * depth < (q + 1) * plane and (s + 1) * depth > q * plane:
                        t = g * GROUP + s
                        pltpu.matmul_acc_lhs(
                            accs[unit][0][t], xl_ref[shifts[t], q + s], reg if first else None
                        )
                        first = False
            if g >= 3:
                place(g - 3)
        for g in range(max(groups - 3, 0), groups):
            place(g)

    def per_disp(ll, carry):
        pltpu.make_async_copy(wbuf.at[ll], wbuf.at[ll], sems.at[ll]).wait()
        start, stop = packed[list_rows, ll], packed[list_rows, ll + 1]

        def per_block(blk, inner):
            base = start + blk * BLOCK
            live = jnp.minimum(stop - base, BLOCK)
            lax.switch(
                (live + GROUP - 1) // GROUP - 1,
                [functools.partial(block_body, ll, base, live, GROUP * (c + 1)) for c in range(BLOCK // GROUP)],
            )
            return inner

        lax.fori_loop(0, (stop - start + BLOCK - 1) // BLOCK, per_block, 0)
        return carry

    lax.fori_loop(0, disp_count, per_disp, 0)
    for r, out_ref in enumerate(out_refs):
        part = pl.ds(r * block_boxes, block_boxes)
        out_ref[...] = sum(total[part] for total in totals).astype(jnp.bfloat16)


def shifted_factors(x_kernels):
    term_count, stacked, order_k = x_kernels.shape
    plane = order_k * order_k
    depth = term_count * order_k
    flat = x_kernels.reshape(term_count, 3, order_k, order_k).transpose(1, 2, 0, 3).reshape(3, order_k, depth)
    padded = jnp.pad(flat, ((0, 0), (0, 0), (plane, plane)))
    parts = {}
    for q in range(GROUP * depth // plane):
        for s in range(GROUP):
            if s * depth < (q + 1) * plane and (s + 1) * depth > q * plane:
                low = plane + q * plane - s * depth
                parts[q + s] = padded[:, :, low : low + plane]
    return jnp.stack([parts[p] for p in range(len(parts))], axis=1)


def convolve(sources, shifted, yz_kernels, packed, dest_count, term_count, order_k):
    plane = order_k * order_k
    block_boxes = sources[0].shape[0]
    disp_count = yz_kernels.shape[1] // (term_count * plane)
    dims = (term_count, order_k, disp_count, len(sources), dest_count)
    tile = jax.ShapeDtypeStruct((block_boxes, order_k, plane), jnp.bfloat16)
    return pl.pallas_call(
        functools.partial(conv_kernel, dims),
        out_shape=[tile] * dest_count,
        in_specs=[SMEM] + [VMEM] * (len(sources) + 1) + [ANY],
        out_specs=[VMEM] * dest_count,
        scratch_shapes=[
            pltpu.VMEM((disp_count, term_count, plane, plane), jnp.bfloat16),
            pltpu.VMEM((BLOCK * term_count * order_k, plane), jnp.bfloat16),
            *[pltpu.VMEM((dest_count * block_boxes + 1, order_k, plane), jnp.float32)] * TOTALS,
            pltpu.VMEM((len(sources) * block_boxes, order_k, plane), jnp.bfloat16),
            pltpu.SemaphoreType.DMA((disp_count,)),
        ],
        compiler_params=pltpu.CompilerParams(vmem_limit_bytes=48 * MIB),
        name="convolve",
    )(packed, *sources, shifted, yz_kernels)


def flips(count, step):
    return [(i, i ^ step) for i in range(count)]


def gather_sources(source, lo_count):
    near = [source] + [lax.ppermute(source, "lo", flips(lo_count, r)) for r in range(1, lo_count)]
    return near + [lax.ppermute(block, "oct", flips(2, 1)) for block in near]


def shards(
    coefficients,
    potential,
    to_values,
    x_kernels,
    yz_kernels,
    two_scale,
    disp_ids,
    dest_box,
    parent_of,
    child_octant,
):
    box_count, slot_count = disp_ids.shape
    order_k = to_values.shape[0]
    plane = order_k * order_k
    term_count = x_kernels.shape[0]
    disp_rows = yz_kernels.shape[1] // (term_count * plane)
    oct_count, hi_count, lo_count = (lax.axis_size(name) for name in ("oct", "hi", "lo"))
    oct_here, hi_here, lo_here = (lax.axis_index(name) for name in ("oct", "hi", "lo"))
    sub_count = hi_count * lo_count
    devices_all = oct_count * sub_count
    info = jnp.stack([oct_here, hi_here, lo_here]).astype(jnp.int32)
    tile = (box_count, order_k, plane)
    peer_tiles = jax.ShapeDtypeStruct((sub_count, order_k, plane), jnp.bfloat16)

    words = pl.pallas_call(
        pack_kernel,
        out_shape=jax.ShapeDtypeStruct((devices_all, box_count // 2, LANES), jnp.int32),
        in_specs=[SMEM] * 2 + [VMEM] * 2,
        out_specs=VMEM,
        name="pack_tables",
    )(parent_of, child_octant, disp_ids, dest_box)
    words, coefficients = lax.optimization_barrier((words, coefficients))
    words = lax.all_to_all(words, ("oct", "hi", "lo"), 0, 0, tiled=True)

    source, send_potential = pl.pallas_call(
        first_kernel,
        out_shape=[jax.ShapeDtypeStruct(tile, jnp.bfloat16), peer_tiles],
        in_specs=[SMEM] + [VMEM] * 3,
        out_specs=[VMEM] * 2,
        scratch_shapes=[pltpu.VMEM(peer_tiles.shape, jnp.float32)],
        name="first_source",
    )(parent_of, coefficients, potential, to_values)

    parents = box_count // 8 * order_k
    source, late_values = lax.optimization_barrier((source, to_values))
    fixed = pl.pallas_call(
        constants_kernel,
        out_shape=[
            pltpu.VMEM((12, 2, plane, plane), jnp.bfloat16),
            jax.ShapeDtypeStruct((parents, 2 * parents), jnp.float32),
            jax.ShapeDtypeStruct((2 * parents, parents), jnp.float32),
        ],
        in_specs=[VMEM] * 2,
        out_specs=[VMEM] * 3,
        compiler_params=pltpu.CompilerParams(vmem_limit_bytes=16 * MIB),
        name="make_constants",
    )(late_values, two_scale)
    fixed = [pltpu.with_memory_space_constraint(fixed[0], pltpu.VMEM)] + list(fixed[1:])

    list_rows = -(-(oct_count * lo_count * box_count * slot_count // LANES + 8) // 8) * 8
    words, fixed = lax.optimization_barrier((words, fixed))
    sort_dims = (oct_count, hi_count, lo_count, box_count, slot_count, disp_rows)
    list_shape = jax.ShapeDtypeStruct((list_rows, LANES), jnp.int32)
    packed, found = pl.pallas_call(
        functools.partial(route_kernel, sort_dims, True),
        out_shape=[list_shape, jax.ShapeDtypeStruct((slot_count + 8, LANES), jnp.int32)],
        in_specs=[SMEM, VMEM],
        out_specs=[VMEM] * 2,
        compiler_params=pltpu.CompilerParams(vmem_limit_bytes=16 * MIB),
        name="route_slots",
    )(info, words)
    came_from = found[slot_count + 1, :box_count] // box_count % sub_count
    shifted = shifted_factors(x_kernels)

    for iteration in range(ITERS):
        last = iteration == ITERS - 1
        sources = gather_sources(source, lo_count)
        outs = convolve(sources, shifted, yz_kernels, packed, hi_count, term_count, order_k)
        if not last:
            own_part, send_potential = lax.optimization_barrier((outs[0], send_potential))
            outs = [own_part] + list(outs[1:])
        parts = [outs[0]] + [lax.ppermute(outs[r], "hi", flips(hi_count, r)) for r in range(1, hi_count)]
        kernel = functools.partial(tree_kernel, last, hi_count)
        if last:
            fields, parents = pl.pallas_call(
                kernel,
                out_shape=[
                    peer_tiles,
                    jax.ShapeDtypeStruct((box_count // 8, order_k * plane), jnp.float32),
                ],
                in_specs=[SMEM] + [VMEM] * (hi_count + 3),
                out_specs=[VMEM] * 2,
                name="last_tree",
            )(came_from, *parts, *fixed)
        else:
            moved_potential = lax.all_to_all(send_potential, ("hi", "lo"), 0, 0, tiled=True)
            source = pl.pallas_call(
                kernel,
                out_shape=jax.ShapeDtypeStruct(tile, jnp.bfloat16),
                in_specs=[SMEM] + [VMEM] * (hi_count + 4),
                out_specs=VMEM,
                name="tree_source",
            )(came_from, *parts, *fixed, moved_potential)
            source, words = lax.optimization_barrier((source, words))
            packed = pl.pallas_call(
                functools.partial(route_kernel, sort_dims, False),
                out_shape=list_shape,
                in_specs=[SMEM, VMEM, VMEM],
                out_specs=VMEM,
                compiler_params=pltpu.CompilerParams(vmem_limit_bytes=16 * MIB),
                name="route_again",
            )(info, words, found)
    returned = lax.all_to_all(fields, ("hi", "lo"), 0, 0, tiled=True)
    next_field = pl.pallas_call(
        unpack_kernel,
        out_shape=jax.ShapeDtypeStruct((box_count, order_k * plane), jnp.float32),
        in_specs=[SMEM, VMEM],
        out_specs=VMEM,
        name="unpack_fields",
    )(parent_of, returned)
    return next_field, parents


def solution(mesh):
    oct_count, sub_count = mesh.devices.shape
    lo_count = 4
    split = Mesh(mesh.devices.reshape(oct_count, sub_count // lo_count, lo_count), ("oct", "hi", "lo"))
    rows = ("oct", "hi", "lo")
    placed = (
        P(rows, None),
        P(rows, None),
        P(),
        P(),
        P(),
        P(),
        P(rows, None),
        P(rows, None),
        P(rows),
        P(rows),
    )
    return jax.shard_map(
        shards,
        mesh=split,
        in_specs=placed,
        out_specs=(P(rows, None), P(rows, None)),
        check_vma=False,
    )
```

```python
import functools

import jax
import jax.numpy as jnp
from jax import lax
from jax.experimental import pallas as pl
from jax.experimental.pallas import tpu as pltpu
from jax.sharding import Mesh
from jax.sharding import PartitionSpec as P

ITERS = 2
BLOCK = 32
TOTALS = 1
GROUP = 4
LANES = 128
MIB = 1024 * 1024
SMEM = pl.BlockSpec(memory_space=pltpu.SMEM)
VMEM = pl.BlockSpec(memory_space=pltpu.VMEM)
ANY = pl.BlockSpec(memory_space=pl.ANY)


def iota(shape, dim):
    return lax.broadcasted_iota(jnp.int32, shape, dim)


def mm(left, right):
    return jnp.dot(left, right, precision=lax.Precision.HIGHEST, preferred_element_type=jnp.float32)


def dot16(left, right):
    return jnp.dot(left, right, preferred_element_type=jnp.float32)


def halves(matrix):
    high = matrix.astype(jnp.bfloat16)
    return high, (matrix - high.astype(jnp.float32)).astype(jnp.bfloat16)


def mm_halves(left, right):
    rows = left[0].shape[0]
    both = dot16(jnp.concatenate(left, axis=0), right[0])
    return both[:rows] + both[rows:] + dot16(left[0], right[1])


def rows_high(matrix):
    order_k, width = matrix.shape
    return jnp.broadcast_to(matrix[:, None, :], (order_k, order_k, width)).reshape(order_k * order_k, width)


def rows_low(matrix):
    order_k, width = matrix.shape
    return jnp.broadcast_to(matrix[None, :, :], (order_k, order_k, width)).reshape(order_k * order_k, width)


def spread_columns(matrix):
    order_k = matrix.shape[0]
    plane = order_k * order_k
    slot, lane = iota((order_k, 2 * plane), 0), iota((order_k, 2 * plane), 1)
    chosen = jnp.where(lane < plane, lane // order_k, lane % order_k) == slot
    rows = jnp.concatenate(halves(matrix) + halves(matrix.T), axis=0)
    wide = dot16(rows, chosen.astype(jnp.float32).astype(jnp.bfloat16))
    plain = wide[:order_k] + wide[order_k : 2 * order_k]
    turned = wide[2 * order_k : 3 * order_k] + wide[3 * order_k :]
    return plain[:, :plane], plain[:, plane:], turned[:, :plane], turned[:, plane:]


def masks(order_k):
    shape = (order_k * order_k, order_k * order_k)
    row, lane = iota(shape, 0), iota(shape, 1)
    return row // order_k, row % order_k, lane // order_k, lane % order_k


def pack_kernel(parent_of, octant, disp_ref, dest_ref, out_ref):
    boxes, slots = disp_ref.shape
    half = boxes // 2
    dest = dest_ref[...]
    entry = jnp.where(dest >= 0, dest * 32 + disp_ref[...] + 1, 0).astype(jnp.float32)
    lane = iota((slots, LANES), 1)
    slot = iota((slots, LANES), 0)
    lane_out = iota((half, LANES), 1)
    row_out = iota((half, LANES), 0)
    words = jnp.zeros((half, LANES), jnp.float32)
    for h in range(2):
        start = h * (LANES // 2)
        words += mm(entry[h * half : (h + 1) * half], (lane == slot + start).astype(jnp.float32))
    words = words.astype(jnp.int32)
    for b in range(boxes):
        here = (row_out == b % half) & (lane_out == b // half * (LANES // 2) + slots)
        words = jnp.where(here, parent_of[b] * 8 + octant[b], words)
    for d in range(out_ref.shape[0]):
        out_ref[d] = words


def first_kernel(parent_of, info, coef_ref, pot_ref, to_ref, *refs):
    *out_refs, rows_ref = refs
    order_k = to_ref.shape[0]
    plane = order_k * order_k
    to_high, to_low, back_high, back_low = spread_columns(to_ref[...])
    row_high, row_low, lane_high, lane_low = masks(order_k)
    value_pair = halves(rows_high(back_high) * rows_low(back_low))
    back_pair = halves(rows_high(to_high) * rows_low(to_low))
    value_x = halves(jnp.where(row_low == lane_low, rows_high(to_high), 0.0))
    source_x = halves(jnp.where(row_high == lane_low, rows_low(back_high), 0.0))

    def by_x(ref):
        return jnp.concatenate([ref[:, x * plane : (x + 1) * plane] for x in range(order_k)], axis=0)

    values = mm_halves(value_x, halves(mm_halves(halves(by_x(coef_ref)), value_pair)))
    product = values * (by_x(pot_ref) + 0.25 * values * values)
    source = mm_halves(source_x, halves(mm_halves(halves(product), back_pair)))
    boxes = pot_ref.shape[0]
    source = source.astype(jnp.bfloat16).reshape(boxes, order_k, plane)
    peers, lo_count = rows_ref.shape[0], len(out_refs)
    if peers > boxes:
        rows_ref[...] = jnp.zeros_like(rows_ref)
    for b in range(boxes):
        peer = parent_of[b] * 8 // boxes % peers
        for x in range(order_k):
            rows_ref[peer, x : x + 1, :] = pot_ref[b : b + 1, x * plane : (x + 1) * plane]
    for r, out_ref in enumerate(out_refs):
        out_ref[:boxes] = source
        for h in range(peers // lo_count):
            out_ref[boxes + h] = rows_ref[h * lo_count + (info[2] ^ r)].astype(jnp.bfloat16)


def route_kernel(dims, first, info, words_ref, *refs):
    oct_count, hi_count, lo_count, boxes, slots, disp_rows = dims
    oct_here, hi_here, lo_here = info[0], info[1], info[2]
    width = LANES // 2
    words = words_ref[...].reshape(-1, LANES)
    table = jnp.concatenate([words[:, :width], words[:, width:]], axis=0)
    total = table.shape[0]

    def box_id(row):
        member = row % (total // 2)
        return member // (boxes // 2) * boxes + row // (total // 2) * (boxes // 2) + member % (boxes // 2)

    place_col, id_col = table[:, slots : slots + 1], box_id(iota((total, 1), 0))
    flat = table.astype(jnp.float32).T.astype(jnp.int32)
    flat = jnp.where(iota(flat.shape, 0) == slots + 1, box_id(iota(flat.shape, 1)), flat)
    low = (flat % 256).astype(jnp.float32).astype(jnp.bfloat16)
    high = (flat // 256).astype(jnp.float32).astype(jnp.bfloat16)

    def look(hit):
        chosen = hit.astype(jnp.float32).astype(jnp.bfloat16)
        return (dot16(low, chosen) + 256.0 * dot16(high, chosen)).astype(jnp.int32)

    lanes = oct_count * lo_count * boxes
    lane = iota((1, lanes), 1)
    member = lane // boxes
    device = ((member // lo_count) ^ oct_here) * (hi_count * lo_count) + hi_here * lo_count
    device = device + ((member % lo_count) ^ lo_here)
    target = device * boxes + lane % boxes
    dest_rows = hi_count * boxes
    source = iota((slots, lanes), 1)
    list_ref = refs[0] if first else refs[1]
    list_rows = list_ref.shape[0]
    upper = (iota((lanes, lanes), 0) < iota((lanes, lanes), 1)).astype(jnp.float32).astype(jnp.bfloat16)
    ones = jnp.ones((lanes, lanes), jnp.bfloat16)
    ranks = disp_rows * slots
    lower = (iota((ranks, ranks), 1) < iota((ranks, ranks), 0)).astype(jnp.float32).astype(jnp.bfloat16)
    if first:
        found = look(id_col == target)
        refs[1][...] = look(place_col == target)[: slots + 8]
    else:
        found = refs[0][...]
    entry = found[:slots] - 1
    dest = jnp.where(entry >= 0, entry // 32, -1)
    disp = jnp.maximum(entry, 0) % 32
    place = jnp.concatenate(
        [look(id_col == dest[s : s + 1])[slots : slots + 1] for s in range(slots)], axis=0
    )
    owner = place // boxes
    keep = (entry >= 0) & (owner // (hi_count * lo_count) == oct_here) & (owner % lo_count == lo_here)
    away = ((owner // lo_count) % hi_count) ^ hi_here
    shift = jnp.zeros_like(disp)
    for c in range(1, 3):
        shift += (disp >= c * disp_rows).astype(jnp.int32)
    row = disp - shift * disp_rows
    member_of = [keep & (row == g) for g in range(disp_rows)]
    marks = jnp.concatenate(member_of, axis=0).astype(jnp.float32).astype(jnp.bfloat16)
    sums = dot16(marks, ones)
    starts = dot16(lower, sums.astype(jnp.bfloat16))
    ordinal = (starts + dot16(marks, upper)).astype(jnp.int32)
    position = jnp.full((slots, lanes), -1, jnp.int32)
    for g in range(disp_rows):
        position = jnp.where(member_of[g], ordinal[g * slots : (g + 1) * slots], position)
    code = (source * 4 + shift) * dest_rows + away * boxes + place % boxes
    pieces = [((code // 256**n) % 256).astype(jnp.float32) for n in range(3)]
    listed = jnp.zeros((3 * list_rows, LANES), jnp.float32)
    for s in range(slots):
        spot = position[s : s + 1]
        in_row = (spot // LANES == iota((list_rows, lanes), 0)) & (spot >= 0)
        left = jnp.concatenate([jnp.where(in_row, piece[s : s + 1], 0.0) for piece in pieces], axis=0)
        in_lane = (spot % LANES == iota((LANES, lanes), 0)).astype(jnp.float32).astype(jnp.bfloat16)
        listed += lax.dot_general(
            left.astype(jnp.bfloat16), in_lane, (((1,), (1,)), ((), ())), preferred_element_type=jnp.float32
        )
    packed = sum(
        listed[n * list_rows : (n + 1) * list_rows].astype(jnp.int32) * 256**n for n in range(3)
    )
    bound = (starts[ranks - 1 : ranks] + sums[ranks - 1 : ranks]).astype(jnp.int32)
    for g in range(disp_rows):
        bound = jnp.where(lane == g, starts[g * slots : g * slots + 1].astype(jnp.int32), bound)
    list_ref[...] = jnp.where(iota(packed.shape, 0) == list_rows - 7, bound, packed)


def constants_kernel(to_ref, two_ref, mats_ref, lift_ref, drop_ref):
    order_k = to_ref.shape[0]
    to_high, to_low, back_high, back_low = spread_columns(to_ref[...])
    spread = [spread_columns(two_ref[c]) for c in range(2)]
    two, flip = [four[:2] for four in spread], [four[2:] for four in spread]
    row_high, row_low, lane_high, lane_low = masks(order_k)
    made = []
    for quad in range(4):
        made.append(rows_high(flip[quad // 2][0]) * rows_low(flip[quad % 2][1]))
    for quad in range(4):
        made.append(rows_high(two[quad // 2][0]) * rows_low(two[quad % 2][1]))
    made.append(rows_high(back_high) * rows_low(back_low))
    made.append(rows_high(to_high) * rows_low(to_low))
    made.append(jnp.where(row_high == lane_high, rows_low(to_low), 0.0))
    made.append(jnp.where(row_high == lane_high, rows_low(back_low), 0.0))
    for n, matrix in enumerate(made):
        mats_ref[n, 0], mats_ref[n, 1] = halves(matrix)
    parents, wide = lift_ref.shape
    shape = (order_k, wide)
    lifted = jnp.zeros(shape, jnp.float32)
    for c in range(2):
        hot = (iota(shape, 1) % order_k == iota(shape, 0)) & ((iota(shape, 1) // order_k) % 2 == c)
        lifted += mm(two_ref[c], hot.astype(jnp.float32))
    lifted = jnp.concatenate([lifted] * (parents // order_k), axis=0)
    lift_ref[...] = jnp.where(
        iota(lift_ref.shape, 0) // order_k == iota(lift_ref.shape, 1) // (2 * order_k), lifted, 0.0
    )
    hot = (iota((order_k, parents), 1) % order_k == iota((order_k, parents), 0)).astype(jnp.float32)
    dropped = jnp.concatenate([mm(two_ref[c].T, hot) for c in range(2)] * (parents // order_k), axis=0)
    drop_ref[...] = jnp.where(
        iota(drop_ref.shape, 0) // (2 * order_k) == iota(drop_ref.shape, 1) // order_k, dropped, 0.0
    )


def tree_kernel(last, part_count, boxes, came_from, info, *refs):
    parts = refs[:part_count]
    mats_ref, lift_ref, drop_ref = refs[part_count : part_count + 3]
    rest = refs[part_count + 3 :]
    gathered = parts[0][:boxes].astype(jnp.float32)
    for part in parts[1:]:
        gathered = gathered + part[:boxes].astype(jnp.float32)
    order_k, plane = gathered.shape[1:]
    parent_count = boxes // 8

    def matrix(n):
        return mats_ref[n, 0], mats_ref[n, 1]

    summed = None
    for quad in range(4):
        stacked = jnp.concatenate(
            [gathered[8 * p + 4 * c + quad] for p in range(parent_count) for c in range(2)], axis=0
        )
        inner = mm_halves(halves(stacked), matrix(quad))
        summed = inner if summed is None else summed + inner
    own = mm_halves(halves(lift_ref[...]), halves(summed))
    dropped_x = halves(mm_halves(halves(drop_ref[...]), halves(own)))
    dropped = [mm_halves(dropped_x, matrix(4 + quad)) for quad in range(4)]
    fields = []
    for b in range(boxes):
        start = (b // 4) * order_k
        fields.append(gathered[b] - dropped[b % 4][start : start + order_k])
    if last:
        field_ref, parent_ref = rest
        if field_ref.shape[0] > boxes:
            field_ref[...] = jnp.zeros_like(field_ref)
        for b in range(boxes):
            field_ref[came_from[b]] = fields[b].astype(field_ref.dtype)
        for p in range(parent_count):
            for i in range(order_k):
                parent_ref[p : p + 1, i * plane : (i + 1) * plane] = own[p * order_k + i : p * order_k + i + 1]
    else:
        out_ref, pot_ref = rest
        lo_count = parts[0].shape[0] - boxes
        for r, part in enumerate(parts):
            pot_ref[r * lo_count : (r + 1) * lo_count] = part[boxes:]
        spots = [
            (came_from[b] // lo_count ^ info[1]) * lo_count + (came_from[b] % lo_count ^ info[2])
            for b in range(boxes)
        ]
        potential = jnp.concatenate([pot_ref[spot] for spot in spots], axis=0).astype(jnp.float32)
        current = halves(jnp.concatenate(fields, axis=0))
        values = mm_halves(matrix(10), halves(mm_halves(current, matrix(8))))
        product = values * (potential + 0.25 * values * values)
        source = mm_halves(matrix(11), halves(mm_halves(halves(product), matrix(9))))
        out_ref[...] = source.astype(jnp.bfloat16).reshape(out_ref.shape)


def unpack_kernel(parent_of, field_ref, out_ref):
    peers, order_k, plane = field_ref.shape
    boxes = out_ref.shape[0]
    for b in range(boxes):
        box = field_ref[parent_of[b] * 8 // boxes % peers].astype(jnp.float32)
        for x in range(order_k):
            out_ref[b : b + 1, x * plane : (x + 1) * plane] = box[x : x + 1]


def conv_kernel(dims, packed, info, *refs):
    term_count, order_k, disp_count, source_count, dest_count, block_boxes = dims
    source_refs = refs[:source_count]
    xl_ref, w_hbm = refs[source_count : source_count + 2]
    out_refs = refs[source_count + 2 : source_count + 2 + dest_count]
    wbuf, pbuf, *totals, held, sems = refs[source_count + 2 + dest_count :]
    plane = order_k * order_k
    list_rows = packed.shape[0] - 7
    half = term_count // 2
    depth = term_count * order_k
    extra = out_refs[0].shape[0] - block_boxes
    dest_rows = dest_count * block_boxes
    def load_row(ll):
        for m in range(term_count):
            column = pl.multiple_of((m * disp_count + ll) * plane, plane)
            pltpu.make_async_copy(w_hbm.at[:, pl.ds(column, plane)], wbuf.at[ll, m], sems.at[ll]).start()

    for ll in range(disp_count):
        load_row(ll)
    for total in totals:
        total[...] = jnp.zeros_like(total)
    for n, ref in enumerate(source_refs):
        held[pl.ds(n * block_boxes, block_boxes)] = ref[:block_boxes]

    def push_w(ll, j, reg):
        for unit in range(2):
            pltpu.matmul_push_rhs(wbuf[ll, unit * half + j], reg, unit)

    def block_body(ll, base, live, slots):
        pl.run_scoped(
            functools.partial(with_accs, ll, base, live, slots),
            *[
                [
                    [pltpu.ACC(unit)((order_k, plane), jnp.float32) for _ in range(slots)]
                    for _ in range(max(2, min(half, 2 * BLOCK // slots)))
                ]
                for unit in range(2)
            ],
        )

    def with_accs(ll, base, live, slots, *accs):
        codes = [packed[(base + t) // LANES, (base + t) % LANES] for t in range(slots)]
        ids = [code // (4 * dest_rows) for code in codes]
        shifts = [(code // dest_rows) % 4 for code in codes]

        stages = len(accs[0])

        def take(j, t):
            for unit in range(2):
                row = (unit * half + j) * order_k + t * depth
                tile = pltpu.matmul_pop(accs[unit][j % stages][t])
                pbuf[row : row + order_k, :] = tile.astype(jnp.bfloat16)

        push_w(ll, 0, 0)
        for j in range(half):
            if j + 1 < half:
                push_w(ll, j + 1, (j + 1) % 2)
            for t in range(slots):
                lhs = held[ids[t]]
                for unit in range(2):
                    pltpu.matmul_acc_lhs(accs[unit][j % stages][t], lhs, j % 2 if t == 0 else None)
                if j + 1 >= stages:
                    take(j + 1 - stages, t)
        for j in range(half - stages + 1, half):
            for t in range(slots):
                take(j, t)

        tiles = GROUP * depth // plane
        groups = slots // GROUP

        def place(g):
            for s in range(GROUP):
                t = g * GROUP + s
                tile = pltpu.matmul_pop(accs[g % 2][0][t])
                total = totals[t % TOTALS]
                dest = jnp.where(t < live, codes[t] % dest_rows, dest_rows)
                total[dest] = total[dest] + tile

        for g in range(groups):
            unit = g % 2
            for q in range(tiles):
                reg = q % 2
                pltpu.matmul_push_rhs(pbuf[pl.ds(g * GROUP * depth + q * plane, plane), :], reg, unit)
                first = True
                for s in range(GROUP):
                    if s * depth < (q + 1) * plane and (s + 1) * depth > q * plane:
                        t = g * GROUP + s
                        pltpu.matmul_acc_lhs(
                            accs[unit][0][t], xl_ref[shifts[t], q + s], reg if first else None
                        )
                        first = False
            if g >= 3:
                place(g - 3)
        for g in range(max(groups - 3, 0), groups):
            place(g)

    def per_disp(ll, carry):
        pltpu.make_async_copy(wbuf.at[ll], wbuf.at[ll], sems.at[ll]).wait()
        start, stop = packed[list_rows, ll], packed[list_rows, ll + 1]

        def per_block(blk, inner):
            base = start + blk * BLOCK
            live = jnp.minimum(stop - base, BLOCK)
            lax.switch(
                (live + GROUP - 1) // GROUP - 1,
                [functools.partial(block_body, ll, base, live, GROUP * (c + 1)) for c in range(BLOCK // GROUP)],
            )
            return inner

        lax.fori_loop(0, (stop - start + BLOCK - 1) // BLOCK, per_block, 0)
        return carry

    lax.fori_loop(0, disp_count, per_disp, 0)
    for r, out_ref in enumerate(out_refs):
        part = pl.ds(r * block_boxes, block_boxes)
        out_ref[:block_boxes] = sum(total[part] for total in totals).astype(jnp.bfloat16)
        for l in range(extra):
            out_ref[block_boxes + l] = source_refs[l][block_boxes + (info[1] ^ r)]


def shifted_factors(x_kernels):
    term_count, stacked, order_k = x_kernels.shape
    plane = order_k * order_k
    depth = term_count * order_k
    flat = x_kernels.reshape(term_count, 3, order_k, order_k).transpose(1, 2, 0, 3).reshape(3, order_k, depth)
    padded = jnp.pad(flat, ((0, 0), (0, 0), (plane, plane)))
    parts = {}
    for q in range(GROUP * depth // plane):
        for s in range(GROUP):
            if s * depth < (q + 1) * plane and (s + 1) * depth > q * plane:
                low = plane + q * plane - s * depth
                parts[q + s] = padded[:, :, low : low + plane]
    return jnp.stack([parts[p] for p in range(len(parts))], axis=1)


def convolve(sources, shifted, yz_kernels, packed, info, dest_count, term_count, order_k, block_boxes, extra):
    plane = order_k * order_k
    disp_count = yz_kernels.shape[1] // (term_count * plane)
    dims = (term_count, order_k, disp_count, len(sources), dest_count, block_boxes)
    tile = jax.ShapeDtypeStruct((block_boxes + extra, order_k, plane), jnp.bfloat16)
    return pl.pallas_call(
        functools.partial(conv_kernel, dims),
        out_shape=[tile] * dest_count,
        in_specs=[SMEM] * 2 + [VMEM] * (len(sources) + 1) + [ANY],
        out_specs=[VMEM] * dest_count,
        scratch_shapes=[
            pltpu.VMEM((disp_count, term_count, plane, plane), jnp.bfloat16),
            pltpu.VMEM((BLOCK * term_count * order_k, plane), jnp.bfloat16),
            *[pltpu.VMEM((dest_count * block_boxes + 1, order_k, plane), jnp.float32)] * TOTALS,
            pltpu.VMEM((len(sources) * block_boxes, order_k, plane), jnp.bfloat16),
            pltpu.SemaphoreType.DMA((disp_count,)),
        ],
        compiler_params=pltpu.CompilerParams(vmem_limit_bytes=48 * MIB),
        name="convolve",
    )(packed, info, *sources, shifted, yz_kernels)


def flips(count, step):
    return [(i, i ^ step) for i in range(count)]


def gather_sources(blocks):
    near = [blocks[0]] + [lax.ppermute(block, "lo", flips(len(blocks), r)) for r, block in enumerate(blocks) if r]
    return near + [lax.ppermute(block, "oct", flips(2, 1)) for block in near]


def shards(
    coefficients,
    potential,
    to_values,
    x_kernels,
    yz_kernels,
    two_scale,
    disp_ids,
    dest_box,
    parent_of,
    child_octant,
):
    box_count, slot_count = disp_ids.shape
    order_k = to_values.shape[0]
    plane = order_k * order_k
    term_count = x_kernels.shape[0]
    disp_rows = yz_kernels.shape[1] // (term_count * plane)
    oct_count, hi_count, lo_count = (lax.axis_size(name) for name in ("oct", "hi", "lo"))
    oct_here, hi_here, lo_here = (lax.axis_index(name) for name in ("oct", "hi", "lo"))
    sub_count = hi_count * lo_count
    devices_all = oct_count * sub_count
    info = jnp.stack([oct_here, hi_here, lo_here]).astype(jnp.int32)
    tile = (box_count, order_k, plane)
    peer_tiles = jax.ShapeDtypeStruct((sub_count, order_k, plane), jnp.bfloat16)

    words = pl.pallas_call(
        pack_kernel,
        out_shape=jax.ShapeDtypeStruct((devices_all, box_count // 2, LANES), jnp.int32),
        in_specs=[SMEM] * 2 + [VMEM] * 2,
        out_specs=VMEM,
        name="pack_tables",
    )(parent_of, child_octant, disp_ids, dest_box)
    words, coefficients = lax.optimization_barrier((words, coefficients))
    words = lax.all_to_all(words, ("oct", "hi", "lo"), 0, 0, tiled=True)

    blocks = pl.pallas_call(
        first_kernel,
        out_shape=[jax.ShapeDtypeStruct((box_count + hi_count, order_k, plane), jnp.bfloat16)] * lo_count,
        in_specs=[SMEM] * 2 + [VMEM] * 3,
        out_specs=[VMEM] * lo_count,
        scratch_shapes=[pltpu.VMEM(peer_tiles.shape, jnp.float32)],
        name="first_source",
    )(parent_of, info, coefficients, potential, to_values)

    parents = box_count // 8 * order_k
    first, late_values = lax.optimization_barrier((blocks[0], to_values))
    blocks = [first] + list(blocks[1:])
    fixed = pl.pallas_call(
        constants_kernel,
        out_shape=[
            pltpu.VMEM((12, 2, plane, plane), jnp.bfloat16),
            jax.ShapeDtypeStruct((parents, 2 * parents), jnp.float32),
            jax.ShapeDtypeStruct((2 * parents, parents), jnp.float32),
        ],
        in_specs=[VMEM] * 2,
        out_specs=[VMEM] * 3,
        compiler_params=pltpu.CompilerParams(vmem_limit_bytes=16 * MIB),
        name="make_constants",
    )(late_values, two_scale)
    fixed = [pltpu.with_memory_space_constraint(fixed[0], pltpu.VMEM)] + list(fixed[1:])

    list_rows = -(-(oct_count * lo_count * box_count * slot_count // LANES + 8) // 8) * 8
    words, fixed = lax.optimization_barrier((words, fixed))
    sort_dims = (oct_count, hi_count, lo_count, box_count, slot_count, disp_rows)
    list_shape = jax.ShapeDtypeStruct((list_rows, LANES), jnp.int32)
    packed, found = pl.pallas_call(
        functools.partial(route_kernel, sort_dims, True),
        out_shape=[list_shape, jax.ShapeDtypeStruct((slot_count + 8, LANES), jnp.int32)],
        in_specs=[SMEM, VMEM],
        out_specs=[VMEM] * 2,
        compiler_params=pltpu.CompilerParams(vmem_limit_bytes=16 * MIB),
        name="route_slots",
    )(info, words)
    came_from = found[slot_count + 1, :box_count] // box_count % sub_count
    shifted = shifted_factors(x_kernels)

    for iteration in range(ITERS):
        last = iteration == ITERS - 1
        outs = convolve(
            gather_sources(blocks),
            shifted,
            yz_kernels,
            packed,
            info,
            hi_count,
            term_count,
            order_k,
            box_count,
            0 if last else lo_count,
        )
        parts = [outs[0]] + [lax.ppermute(outs[r], "hi", flips(hi_count, r)) for r in range(1, hi_count)]
        kernel = functools.partial(tree_kernel, last, hi_count, box_count)
        if last:
            fields, parents = pl.pallas_call(
                kernel,
                out_shape=[
                    peer_tiles,
                    jax.ShapeDtypeStruct((box_count // 8, order_k * plane), jnp.float32),
                ],
                in_specs=[SMEM] * 2 + [VMEM] * (hi_count + 3),
                out_specs=[VMEM] * 2,
                name="last_tree",
            )(came_from, info, *parts, *fixed)
        else:
            source = pl.pallas_call(
                kernel,
                out_shape=jax.ShapeDtypeStruct(tile, jnp.bfloat16),
                in_specs=[SMEM] * 2 + [VMEM] * (hi_count + 3),
                out_specs=VMEM,
                scratch_shapes=[pltpu.VMEM(peer_tiles.shape, jnp.bfloat16)],
                name="tree_source",
            )(came_from, info, *parts, *fixed)
            source, words = lax.optimization_barrier((source, words))
            blocks = [source] * lo_count
            packed = pl.pallas_call(
                functools.partial(route_kernel, sort_dims, False),
                out_shape=list_shape,
                in_specs=[SMEM, VMEM, VMEM],
                out_specs=VMEM,
                compiler_params=pltpu.CompilerParams(vmem_limit_bytes=16 * MIB),
                name="route_again",
            )(info, words, found)
    returned = lax.all_to_all(fields, ("hi", "lo"), 0, 0, tiled=True)
    next_field = pl.pallas_call(
        unpack_kernel,
        out_shape=jax.ShapeDtypeStruct((box_count, order_k * plane), jnp.float32),
        in_specs=[SMEM, VMEM],
        out_specs=VMEM,
        name="unpack_fields",
    )(parent_of, returned)
    return next_field, parents


def solution(mesh):
    oct_count, sub_count = mesh.devices.shape
    lo_count = 4
    split = Mesh(mesh.devices.reshape(oct_count, sub_count // lo_count, lo_count), ("oct", "hi", "lo"))
    rows = ("oct", "hi", "lo")
    placed = (
        P(rows, None),
        P(rows, None),
        P(),
        P(),
        P(),
        P(),
        P(rows, None),
        P(rows, None),
        P(rows),
        P(rows),
    )
    return jax.shard_map(
        shards,
        mesh=split,
        in_specs=placed,
        out_specs=(P(rows, None), P(rows, None)),
        check_vma=False,
    )
```
